128 devices in a mesh: lat: 16 (over y_hi, z, core), wave: 8 (over x, y_lo).
Axes of the slice: x: 4, y: 4 (y_hi: 2, y_lo: 2; y = y_hi * 2 + y_lo), z: 4, core: 2. Of those that a mesh axis runs over, the one named last changes fastest.
Arguments:
- grad_grid: float32 [3, 6, 640, 2560], P(None, None, ('lat', 'wave')), may hold values from -6 to 6
- owner: int32 [640], replicated, may hold values from 0 to 639, each once
- legendre: float32 [640, 640, 1408], P('wave', 'lat'), may hold values from -0.25 to 0.25
- lat_weights: float32 [640], P('lat'), may hold values from 0.5 to 2
- modes_e: float32 [6, 6], replicated, may hold values from -2.5 to 2.5
- modes_f: float32 [6, 6], replicated, may hold values from -2.5 to 2.5
- rates: float32 [6], replicated, may hold values from 0.1 to 10
- height_matrix: float32 [6, 6], replicated, may hold values from -2.5 to 2.5
- heating_matrix: float32 [6, 6], replicated, may hold values from -2.5 to 2.5
Outputs:
- grad_out: float32 [3, 6, 640, 2560], P(None, None, ('lat', 'wave'))
The draws below stay inside these ranges and needn't reach their ends.
Inputs may be any that keep to these rules, and one draw needn't show every extreme that they name: Each pair number appears once; slot j holds the wavenumbers owner[j] and 1279 - owner[j].
All inputs are finite; a program needn't handle non-finite values.
Results may differ from the reference program's by a relative error of at most 0.0001.
Values sent between devices are 32-bit elements; how exact they have to be, the bound alone decides.
No kernel may reach another device: no remote copies, remote signals or barrier semaphores. Data moves between devices by JAX's collectives and lax.ppermute only.
A program may use at most 256 MiB of HBM per device.

```python
import math
import jax
import jax.numpy as jnp
from jax import lax

NLON = 2560
LEV = 6
PAIRS = 640
PACK = 1408
NLAT = 640
N_WAVE = 8


def level_of(stream_key, shape, cuts, low, largest):
    level, own = 1.0, jax.random.fold_in(stream_key, 6)
    for position, parts in cuts:
        draws = jnp.exp(jax.random.uniform(jax.random.fold_in(own, position), (parts,), jnp.float32, low / len(cuts), largest / len(cuts)))
        level = level * jnp.repeat(draws, shape[position] // parts).reshape([-1 if axis == position else 1 for axis in range(len(shape))])
    return level


def bell_draw(rng, extent, scale, limit, split=(), kind=jnp.bfloat16):
    gain = level_of(rng, extent, split, -0.22, 0.18) if split else 1.0
    entries = jax.random.normal(rng, extent, jnp.float32) * scale * gain
    return jnp.minimum(jnp.maximum(entries, -limit), limit).astype(kind)


def setup_inputs(seed: int = 0) -> dict:
    keys = jax.random.split(jax.random.key(seed), 10)
    grad_grid = bell_draw(keys[0], (3, LEV, NLAT, NLON), 1.0, 6.0, ((2, 128),), jnp.float32)
    owner = jax.random.permutation(keys[1], PAIRS).astype(jnp.int32)
    legendre = bell_draw(keys[2], (PAIRS, NLAT, PACK), NLAT ** -0.5, 0.25, ((0, 8), (1, 16)), jnp.float32)
    lat_weights = jnp.clip(jnp.exp(math.log(2.0) - 1.3862944 * jax.random.uniform(keys[3], (NLAT,), jnp.float32) ** level_of(keys[3], (NLAT,), ((0, 16),), -0.2, 0.2)), 0.5, 2.0)
    modes_e = bell_draw(keys[4], (LEV, LEV), LEV ** -0.5, 2.5, (), jnp.float32)
    modes_f = bell_draw(keys[5], (LEV, LEV), LEV ** -0.5, 2.5, (), jnp.float32)
    rates = jnp.clip(jnp.exp(jax.random.uniform(keys[6], (LEV,), jnp.float32, math.log(0.1), math.log(10.0))), 0.1, 10.0)
    height_matrix = bell_draw(keys[7], (LEV, LEV), LEV ** -0.5, 2.5, (), jnp.float32)
    heating_matrix = bell_draw(keys[8], (LEV, LEV), LEV ** -0.5, 2.5, (), jnp.float32)
    return {"grad_grid": grad_grid, "owner": owner, "legendre": legendre, "lat_weights": lat_weights, "modes_e": modes_e, "modes_f": modes_f, "rates": rates, "height_matrix": height_matrix, "heating_matrix": heating_matrix}


TOP_HARMONIC = lax.Precision.HIGHEST

def fourier_table(lon_count, truncation):
    lon_index = lax.broadcasted_iota(jnp.int32, (lon_count, truncation), 0)
    wave_index = lax.broadcasted_iota(jnp.int32, (lon_count, truncation), 1)
    phases = (lon_index * wave_index % lon_count).astype(jnp.float32) * (2.0 * math.pi / lon_count)
    factor = math.sqrt(2.0 / lon_count)
    return jnp.concatenate([jnp.cos(phases) * factor, -jnp.sin(phases) * factor], axis=1)

def slot_masks(first_wave, slot_start, slot_count, truncation):
    packed = slot_start + lax.broadcasted_iota(jnp.int32, (slot_count, first_wave.shape[0]), 0)
    is_first = packed < truncation - first_wave[None, :]
    is_second = jnp.logical_and(jnp.logical_not(is_first), packed <= truncation)
    degree = jnp.where(is_first, first_wave[None, :] + packed, packed - 1)
    return (is_first, is_second, degree)

def legendre_terms(leg_table, fourier, first_wave, slot_start, slot_count, truncation):
    table_block = lax.dynamic_slice_in_dim(leg_table, slot_start, slot_count, 2)
    is_first, is_second, degree = slot_masks(first_wave, slot_start, slot_count, truncation)
    first_part = jnp.einsum('plk,flrp->kpfr', table_block, fourier[:, :, 0:2, :], precision=TOP_HARMONIC)
    second_part = jnp.einsum('plk,flrp->kpfr', table_block, fourier[:, :, 2:4, :], precision=TOP_HARMONIC)
    return jnp.where(is_first[:, :, None, None], first_part, jnp.where(is_second[:, :, None, None], second_part, 0.0))

def semi_implicit(harmonic_coefficient_arrays, degree, truncation, modes_e, modes_f, rates, height_matrix, heating_matrix):
    levels = modes_e.shape[0]
    state_variables = harmonic_coefficient_arrays.reshape(harmonic_coefficient_arrays.shape[0], harmonic_coefficient_arrays.shape[1], 3, levels, 2)
    vorticity = state_variables[:, :, 0]
    spreading_rate = state_variables[:, :, 1]
    thermal_state = state_variables[:, :, 2]
    degree_float = degree.astype(jnp.float32)
    harmonic_order_factor = (degree_float * (degree_float + 1.0) / float(truncation * (truncation + 1)))[:, :, None, None]
    driving_sources = spreading_rate - jnp.einsum('em,zhek->zhmk', heating_matrix, thermal_state, precision=TOP_HARMONIC)
    modal_part = jnp.einsum('em,zhek->zhmk', modes_e, driving_sources, precision=TOP_HARMONIC)
    modal_part = modal_part / (1.0 + 4.0 * harmonic_order_factor * rates[None, None, :, None])
    next_spreading_rate = jnp.einsum('em,zhek->zhmk', modes_f, modal_part, precision=TOP_HARMONIC)
    next_thermal_state = thermal_state - harmonic_order_factor * jnp.einsum('em,zhek->zhmk', height_matrix, next_spreading_rate, precision=TOP_HARMONIC)
    next_rotation = vorticity / (1.0 + 4.0 * harmonic_order_factor * harmonic_order_factor)
    return jnp.stack([next_rotation, next_spreading_rate, next_thermal_state], axis=2).reshape(harmonic_coefficient_arrays.shape)

def legendre_back(leg_table, harmonic_coefficient_arrays, first_wave, slot_start, truncation):
    slot_count = harmonic_coefficient_arrays.shape[0]
    table_block = lax.dynamic_slice_in_dim(leg_table, slot_start, slot_count, 2)
    is_first, is_second, degree = slot_masks(first_wave, slot_start, slot_count, truncation)
    first_back = jnp.einsum('plk,kpfr->flrp', table_block, jnp.where(is_first[:, :, None, None], harmonic_coefficient_arrays, 0.0), precision=TOP_HARMONIC)
    second_back = jnp.einsum('plk,kpfr->flrp', table_block, jnp.where(is_second[:, :, None, None], harmonic_coefficient_arrays, 0.0), precision=TOP_HARMONIC)
    return (first_back, second_back)

def reference(grad_grid, owner, legendre, lat_weights, modes_e, modes_f, rates, height_matrix, heating_matrix):
    state_variables, levels, lat_count, lon_count = grad_grid.shape
    truncation = 2 * owner.shape[0]
    width = state_variables * levels
    dft_table = fourier_table(lon_count, truncation)
    fourier = jnp.dot(grad_grid.reshape(width * lat_count, lon_count), dft_table, precision=TOP_HARMONIC, preferred_element_type=jnp.float32)
    fourier = fourier.reshape(width, lat_count, 2, truncation)
    selected = jnp.concatenate([fourier[..., owner], fourier[..., truncation - 1 - owner]], axis=2)
    packed = legendre.shape[2]
    group = PAIRS // N_WAVE
    pieces = []
    for index in range(N_WAVE):
        pairs_here = owner[index * group:(index + 1) * group]
        table_here = legendre[index * group:(index + 1) * group]
        harmonic_coefficient_arrays = legendre_terms(table_here, selected[..., index * group:(index + 1) * group], pairs_here, 0, packed, truncation)
        is_first, is_second, degree = slot_masks(pairs_here, 0, packed, truncation)
        harmonic_coefficient_arrays = semi_implicit(harmonic_coefficient_arrays, degree, truncation, modes_e, modes_f, rates, height_matrix, heating_matrix)
        first_back, second_back = legendre_back(table_here, harmonic_coefficient_arrays, pairs_here, 0, truncation)
        pieces.append(jnp.concatenate([first_back, second_back], axis=2))
    weighted = jnp.concatenate(pieces, axis=3) * lat_weights[None, :, None, None]
    spectral = jnp.zeros((width, lat_count, 2, truncation), jnp.float32)
    spectral = spectral.at[..., owner].set(weighted[:, :, 0:2, :])
    spectral = spectral.at[..., truncation - 1 - owner].set(weighted[:, :, 2:4, :])
    gridded = lax.dot_general(spectral.reshape(width * lat_count, 2 * truncation), dft_table, (((1,), (1,)), ((), ())), precision=TOP_HARMONIC, preferred_element_type=jnp.float32)
    return gridded.reshape(state_variables, levels, lat_count, lon_count)
```

```python
import math

import jax
import jax.numpy as jnp
import numpy as np
from jax import lax
from jax.experimental import pallas as pl
from jax.experimental.pallas import tpu as pltpu
from jax.sharding import Mesh, PartitionSpec as P

NLON = 2560
NM = 1280
PAIRS = 640
LAT = 640
PACK = 1408
FL = 18
ROWS = 5
N1 = 20
N2 = 128
HALF = 40
BF = jnp.bfloat16
F32 = jnp.float32
CHUNKS = ((0, 10),)
VMEM_BYTES = 40 * 1024 * 1024


def split(x):
    high = x.astype(BF)
    return high, (x - high.astype(F32)).astype(BF)


def dot3(x, weight_high, weight_low, dims):
    high, low = split(x)
    out = lax.dot_general(high, weight_high, dims, preferred_element_type=F32)
    out += lax.dot_general(low, weight_high, dims, preferred_element_type=F32)
    return out + lax.dot_general(high, weight_low, dims, preferred_element_type=F32)


NN = (((1,), (0,)), ((), ()))
NT = (((1,), (1,)), ((), ()))


def constant_tables():
    scale = math.sqrt(2.0 / NLON)
    wave1 = np.arange(N1)[:, None]
    lon2 = np.arange(N2)[None, :]
    turn = 2.0 * np.pi * ((wave1 * lon2) % NLON) / NLON
    twiddle = np.stack([np.cos(turn), np.sin(turn)]).astype(np.float32)
    angle = 2.0 * np.pi * ((np.arange(N2)[:, None] * np.arange(64)[None, :]) % N2) / N2
    cos, sin = np.cos(angle) * scale, np.sin(angle) * scale
    zero = np.zeros_like(cos)
    forward = np.concatenate(
        [
            np.concatenate([cos, zero, -sin, zero], 1),
            np.concatenate([sin, zero, cos, zero], 1),
            np.concatenate([zero, cos, zero, -sin], 1),
            np.concatenate([zero, sin, zero, cos], 1),
        ],
        0,
    ).astype(np.float32)
    backward = np.concatenate(
        [
            np.concatenate([cos.T, sin.T, zero.T, zero.T], 1),
            np.concatenate([zero.T, zero.T, cos.T, sin.T], 1),
            np.concatenate([-sin.T, cos.T, zero.T, zero.T], 1),
            np.concatenate([zero.T, zero.T, -sin.T, cos.T], 1),
        ],
        0,
    ).astype(np.float32)

    def parts(table):
        high = table.astype(jnp.bfloat16)
        return high, (table - high.astype(np.float32)).astype(jnp.bfloat16)

    return twiddle, parts(forward), parts(backward)


def lane_waves():
    lane = lax.broadcasted_iota(jnp.int32, (1, NM), 1)
    return 2 * (lane // N2) + (lane % N2) // 64 + N1 * (lane % 64)


def one_hot(owner_ref, block, rows):
    column = owner_ref[pl.ds(pl.multiple_of(block * rows, rows), rows), 0:1]
    waves = lane_waves()
    second = jnp.where(NM - 1 - column == waves, 1.0, 0.0).astype(BF)
    first = jnp.where(column == waves, 1.0, 0.0).astype(BF)
    return jnp.concatenate([second, first], axis=0)


def fourier_kernel(grid_ref, owner_ref, twiddle_ref, high_ref, low_ref, send_ref, stage_ref, wide_ref):
    for r in range(ROWS):
        tiles = [grid_ref[:, r, N2 * x1 : N2 * (x1 + 1)] for x1 in range(N1)]
        sums = [tiles[x1] + tiles[x1 + 10] for x1 in range(10)]
        differences = [tiles[x1] - tiles[x1 + 10] for x1 in range(10)]
        for m1 in range(11):
            source = sums if m1 % 2 == 0 else differences
            real, imag = source[0], None
            for x1 in range(1, 10):
                turn = 2.0 * math.pi * ((m1 * x1) % N1) / N1
                cos, sin = math.cos(turn), math.sin(turn)
                real = real + source[x1] * cos
                if m1 % 10:
                    term = source[x1] * (-sin)
                    imag = term if imag is None else imag + term
            if imag is None:
                imag = jnp.zeros_like(real)
            for wave, sign in ((m1, 1.0), (N1 - m1, -1.0)):
                if wave in (m1, N1) and sign < 0:
                    continue
                cos = twiddle_ref[0, wave : wave + 1, :]
                sin = twiddle_ref[1, wave : wave + 1, :]
                rotated_real = real * cos + (sign * imag) * sin
                rotated_imag = (sign * imag) * cos - real * sin
                base = (wave % 2) * 256
                stage_ref[wave // 2, r * 24 : r * 24 + FL, base : base + N2] = rotated_real
                stage_ref[wave // 2, r * 24 : r * 24 + FL, base + N2 : base + 256] = rotated_imag
    wide_ref[...] = jnp.zeros_like(wide_ref)
    for t in range(N1 // 2):
        out = dot3(stage_ref[t], high_ref[...], low_ref[...], NN)
        for r in range(ROWS):
            rows = out[r * 24 : r * 24 + FL]
            both = jnp.concatenate([rows[:, :N2], rows[:, N2:]], axis=0)
            wide_ref[r * 40 : r * 40 + 36, t * N2 : (t + 1) * N2] = both
    high, low = split(wide_ref[...])

    def block_step(block, carry):
        picks = one_hot(owner_ref, block, 160)
        out = lax.dot_general(picks, high, NT, preferred_element_type=F32)
        out += lax.dot_general(picks, low, NT, preferred_element_type=F32)
        for r in range(ROWS):
            lanes = out[:, r * 40 : (r + 1) * 40]
            tile = jnp.concatenate([lanes[:160], lanes[160:], jnp.zeros((160, 48), F32)], axis=1)
            for w in range(2):
                for c in range(2):
                    start = w * 80 + c * 40
                    send_ref[c * 8 + block * 2 + w, r] = tile[start : start + 40]
        return carry

    lax.fori_loop(0, 4, block_step, 0)


def inverse_kernel(got_ref, owner_ref, weight_ref, place_ref, twiddle_ref, high_ref, low_ref, out_ref, stage_ref, wide_ref):
    wide_ref[...] = jnp.zeros_like(wide_ref)
    wave = place_ref[1]

    def block_step(block, carry):
        picks = one_hot(owner_ref, block, 160)
        seconds, firsts = [], []
        for r in range(ROWS):
            pieces = [got_ref[c * 8 + block * 2 + w, r] for w in range(2) for c in range(2)]
            tile = jnp.concatenate(pieces, axis=0) * weight_ref[wave * ROWS + r]
            seconds.append(tile[:, 0:40])
            firsts.append(tile[:, 40:80])
        pad = [jnp.zeros((160, 56), F32)]
        both = jnp.concatenate(
            [jnp.concatenate(seconds + pad, axis=1), jnp.concatenate(firsts + pad, axis=1)], axis=0
        )
        high, low = split(both.T)
        out = lax.dot_general(high, picks, NN, preferred_element_type=F32)
        out += lax.dot_general(low, picks, NN, preferred_element_type=F32)
        wide_ref[...] += out
        return carry

    lax.fori_loop(0, 4, block_step, 0)
    for t in range(N1 // 2):
        rows = []
        for r in range(ROWS):
            block = wide_ref[r * 40 : (r + 1) * 40, t * N2 : (t + 1) * N2]
            real = jnp.concatenate([block[:FL], jnp.zeros((6, N2), F32)], axis=0)
            imag = jnp.concatenate([block[FL : 2 * FL], jnp.zeros((6, N2), F32)], axis=0)
            rows.append(jnp.concatenate([real, imag], axis=1))
        out = dot3(jnp.concatenate(rows, axis=0), high_ref[...], low_ref[...], NN)
        for odd in range(2):
            m1 = 2 * t + odd
            real = out[:, odd * 256 : odd * 256 + N2]
            imag = out[:, odd * 256 + N2 : odd * 256 + 256]
            cos = twiddle_ref[0, m1 : m1 + 1, :]
            sin = twiddle_ref[1, m1 : m1 + 1, :]
            stage_ref[m1, :, :N2] = real * cos - imag * sin
            stage_ref[m1, :, N2:] = real * sin + imag * cos
    for r in range(ROWS):
        rows = slice(r * 24, (r + 1) * 24)
        zero, ten = stage_ref[0, rows, :N2], stage_ref[10, rows, :N2]
        sums, gaps = [None], [None]
        for m in range(1, 10):
            sums.append(stage_ref[m, rows, :N2] + stage_ref[N1 - m, rows, :N2])
            gaps.append(stage_ref[m, rows, N2:] - stage_ref[N1 - m, rows, N2:])
        for x1 in range(10):
            even = zero + ten if x1 % 2 == 0 else zero - ten
            odd = jnp.zeros_like(zero)
            for m in range(1, 10):
                turn = 2.0 * math.pi * ((m * x1) % N1) / N1
                term = sums[m] * math.cos(turn) - gaps[m] * math.sin(turn)
                if m % 2 == 0:
                    even = even + term
                else:
                    odd = odd + term
            out_ref[:, r, x1 * N2 : (x1 + 1) * N2] = (even + odd)[:FL]
            out_ref[:, r, (x1 + 10) * N2 : (x1 + 11) * N2] = (even - odd)[:FL]


def spectra_kernel(start, count, place_ref, owner_ref, own_ref, other_ref, four_ref, out_ref):
    target, step = pl.program_id(0), pl.program_id(1)
    core, wave = place_ref[0], place_ref[1]
    extra = count * 36

    @pl.when(step == 0)
    def _():
        out_ref[0, extra : extra + 8, :] = jnp.zeros((8, NM), F32)

    lane = lax.broadcasted_iota(jnp.int32, (1, NM), 1)
    narrow = lax.broadcasted_iota(jnp.int32, (1, N2), 1)
    kept = []
    for i in range(2):
        pair = target * 10 + start + 2 * step + i
        first_wave = owner_ref[wave * 80 + core * HALF + pair]
        mine = four_ref[pl.ds(core * 1600 + pair, HALF, stride=HALF), :]
        theirs = four_ref[pl.ds((1 - core) * 1600 + pair, HALF, stride=HALF), :]
        four = jnp.concatenate([mine, theirs], axis=0)
        four_high = four.astype(BF).astype(F32)
        left = jnp.concatenate([four_high, four_high, four - four_high], axis=0).T
        table = jnp.concatenate([own_ref[i], other_ref[i]], axis=0)
        main = table[:, :NM]
        main_high = main.astype(BF).astype(F32)
        right = jnp.concatenate([main_high, main - main_high, main_high], axis=0)
        both = lax.dot_general(left[:80].astype(BF), right.astype(BF), NN, preferred_element_type=F32)
        kept.append(jnp.where(lane < NM - first_wave, both[40:80], both[0:40])[:36])
        last = jnp.sum(table[:, NM : NM + 1] * four, axis=0, keepdims=True)
        spot = pl.multiple_of((2 * step + i) * N2, N2)
        out_ref[0, extra : extra + 1, pl.ds(spot, N2)] = jnp.where(narrow < 36, last, 0.0)
    out_ref[0, pl.ds(pl.multiple_of(step * 72, 8), 72), :] = jnp.concatenate(kept, axis=0)


def implicit_rows(load, degree, modes_e, modes_f, rates, height, heating):
    q = degree * (degree + 1.0) / float(NM * (NM + 1))
    rotation = 1.0 / (1.0 + 4.0 * q * q)
    damping = [1.0 / (1.0 + 4.0 * q * rates[i]) for i in range(6)]
    out = []
    for part in range(2):
        base = part * FL
        d = [load(base + 6 + l) for l in range(6)]
        t = [load(base + 12 + l) for l in range(6)]
        forced = []
        for l in range(6):
            total = d[l]
            for h in range(6):
                total = total - heating[h * 6 + l] * t[h]
            forced.append(total)
        modal = []
        for i in range(6):
            total = modes_e[i] * forced[0]
            for h in range(1, 6):
                total = total + modes_e[h * 6 + i] * forced[h]
            modal.append(total * damping[i])
        spread = []
        for l in range(6):
            total = modes_f[l] * modal[0]
            for i in range(1, 6):
                total = total + modes_f[i * 6 + l] * modal[i]
            spread.append(total)
        out += [load(base + l) * rotation for l in range(6)]
        out += spread
        for l in range(6):
            total = height[l] * spread[0]
            for h in range(1, 6):
                total = total + height[h * 6 + l] * spread[h]
            out.append(t[l] - q * total)
    return out


def implicit_kernel(start, count, place_ref, owner_ref, e_ref, f_ref, rate_ref, height_ref, heat_ref, x_ref, y_ref, out_ref):
    core, wave, z = place_ref[0], place_ref[1], place_ref[2]
    matrices = [[ref[i] for i in range(36)] for ref in (e_ref, f_ref)]
    rates = [rate_ref[i] for i in range(6)]
    heights = [[ref[i] for i in range(36)] for ref in (height_ref, heat_ref)]
    arguments = (matrices[0], matrices[1], rates, heights[0], heights[1])
    row = lax.broadcasted_iota(jnp.int32, (count, 1), 0)
    first_wave = jnp.zeros((count, 1), jnp.int32)
    for i in range(count):
        value = owner_ref[wave * 80 + core * HALF + z * 10 + start + i]
        first_wave = jnp.where(row == i, value, first_wave)

    tile = pl.program_id(0)
    packed = tile * N2 + lax.broadcasted_iota(jnp.int32, (count, N2), 1)
    degree = jnp.where(packed < NM - first_wave, first_wave + packed, packed - 1).astype(F32)

    def load(j):
        spot = pl.ds(j, count, stride=36)
        return x_ref[spot, :] + y_ref[spot, :]

    for j, value in enumerate(implicit_rows(load, degree, *arguments)):
        out_ref[pl.ds(j, count, stride=36), :] = value
    extra = count * 36
    line = x_ref[extra : extra + 1, :] + y_ref[extra : extra + 1, :]
    flipped = jnp.broadcast_to(line, (8, N2)).T
    degree = jnp.full((1, 8), NM - 1.0, F32)
    values = implicit_rows(lambda j: flipped[j : j + 1], degree, *arguments)
    values.append(jnp.zeros((N2 - 36, 8), F32))
    out_ref[extra : extra + 8, :] = jnp.concatenate(values, axis=0).T


def grid_rows_kernel(start, count, place_ref, owner_ref, own_ref, other_ref, spec_ref, out_ref):
    target, step = pl.program_id(0), pl.program_id(1)
    core, wave = place_ref[0], place_ref[1]
    extra = count * 36
    lane = lax.broadcasted_iota(jnp.int32, (1, NM), 1)
    block = spec_ref[0, pl.ds(pl.multiple_of(step * 72, 8), 72), :]
    pad = jnp.zeros((4, NM), F32)
    for i in range(2):
        pair = target * 10 + start + 2 * step + i
        first_wave = owner_ref[wave * 80 + core * HALF + pair]
        values = jnp.concatenate([block[i * 36 : i * 36 + 36], pad], axis=0)
        is_first = lane < NM - first_wave
        both = jnp.concatenate(
            [jnp.where(is_first, 0.0, values), jnp.where(is_first, values, 0.0)], axis=0
        )
        high, low = split(both)
        table = jnp.concatenate([own_ref[i], other_ref[i]], axis=0)
        back = dot3(table[:, :NM], high, low, NT)
        back = jnp.concatenate([back, jnp.zeros((80, 48), F32)], axis=1)
        spot = pl.multiple_of((2 * step + i) * N2, N2)
        last = spec_ref[0, extra : extra + 1, pl.ds(spot, N2)]
        back = back + table[:, NM : NM + 1] * last
        out_ref[pl.ds(core * 1600 + pair, HALF, stride=HALF), :] = back[:HALF]
        out_ref[pl.ds((1 - core) * 1600 + pair, HALF, stride=HALF), :] = back[HALF:]


def parameters():
    return pltpu.CompilerParams(vmem_limit_bytes=VMEM_BYTES)


def whole(space=pltpu.VMEM):
    return pl.BlockSpec(memory_space=space)


def cost(flops, size):
    return pl.CostEstimate(flops=int(flops), bytes_accessed=int(size), transcendentals=0)


def per_device(
    grad_grid, owner, legendre, lat_weights, modes_e, modes_f, rates, height_matrix, heating_matrix
):
    core, wave, z = lax.axis_index("core"), lax.axis_index("wave"), lax.axis_index("z")
    twiddle, forward, backward = constant_tables()
    smem = whole(pltpu.SMEM)
    place = jnp.stack([core, wave, z]).astype(jnp.int32)
    owner_column = jnp.broadcast_to(owner[:, None], (PAIRS, N2))

    away = lax.dynamic_slice(legendre, ((1 - core) * HALF, 0, 0), (HALF, HALF, PACK))
    other = lax.ppermute(away, "core", [(0, 1), (1, 0)])

    four = pl.pallas_call(
        fourier_kernel,
        out_shape=jax.ShapeDtypeStruct((16, ROWS, HALF, N2), F32),
        in_specs=[whole()] * 5,
        out_specs=whole(),
        scratch_shapes=[pltpu.VMEM((10, 120, 512), F32), pltpu.VMEM((208, NM), F32)],
        compiler_params=parameters(),
        cost_estimate=cost(4e9, 8e6),
        name="fourier",
    )(grad_grid.reshape(FL, ROWS, NLON), owner_column, twiddle, *forward)
    four = lax.all_to_all(four, ("core", "wave"), 0, 0, tiled=True).reshape(3200, N2)

    def table_specs(start):
        return [
            pl.BlockSpec(
                (2, HALF, PACK),
                lambda t, s, place, owner: (place[0] * 20 + t * 5 + start // 2 + s, 0, 0),
            ),
            pl.BlockSpec((2, HALF, PACK), lambda t, s, place, owner: (t * 5 + start // 2 + s, 0, 0)),
        ]

    results = []
    for start, count in CHUNKS:
        height = count * 36 + 8
        spectra = pl.pallas_call(
            lambda *refs: spectra_kernel(start, count, *refs),
            out_shape=jax.ShapeDtypeStruct((4, height, NM), F32),
            grid_spec=pltpu.PrefetchScalarGridSpec(
                num_scalar_prefetch=2,
                grid=(4, count // 2),
                in_specs=table_specs(start)
                + [pl.BlockSpec((3200, N2), lambda t, s, place, owner: (0, 0))],
                out_specs=pl.BlockSpec((1, height, NM), lambda t, s, place, owner: (t, 0, 0)),
            ),
            compiler_params=parameters(),
            cost_estimate=cost(2e9, 2e7),
            name="spectra",
        )(place, owner, legendre, other, four)
        mine = lax.psum_scatter(spectra, "z", scatter_dimension=0, tiled=True).reshape(height, NM)
        theirs = lax.ppermute(mine, "yh", [(0, 1), (1, 0)])
        updated = pl.pallas_call(
            lambda *refs: implicit_kernel(start, count, *refs),
            out_shape=jax.ShapeDtypeStruct((height, NM), F32),
            grid=(10,),
            in_specs=[smem] * 7 + [pl.BlockSpec((height, N2), lambda t: (0, t))] * 2,
            out_specs=pl.BlockSpec((height, N2), lambda t: (0, t)),
            compiler_params=parameters(),
            cost_estimate=cost(1e8, 6e6),
            name="implicit",
        )(
            place,
            owner,
            modes_e.reshape(36),
            modes_f.reshape(36),
            rates,
            height_matrix.reshape(36),
            heating_matrix.reshape(36),
            mine,
            theirs,
        )
        gathered = lax.all_gather(updated[None], "z", axis=0, tiled=True)
        results.append(
            pl.pallas_call(
                lambda *refs: grid_rows_kernel(start, count, *refs),
                out_shape=jax.ShapeDtypeStruct((3200, N2), F32),
                grid_spec=pltpu.PrefetchScalarGridSpec(
                    num_scalar_prefetch=2,
                    grid=(4, count // 2),
                    in_specs=table_specs(start)
                    + [pl.BlockSpec((1, height, NM), lambda t, s, place, owner: (t, 0, 0))],
                    out_specs=pl.BlockSpec((3200, N2), lambda t, s, place, owner: (0, 0)),
                ),
                compiler_params=parameters(),
                cost_estimate=cost(3e9, 2e7),
                name="grid_rows",
            )(place, owner, legendre, other, gathered)
        )
    rows = results[0].reshape(16, ROWS, HALF, N2)
    rows = lax.all_to_all(rows, ("core", "wave"), 0, 0, tiled=True)
    out = pl.pallas_call(
        inverse_kernel,
        out_shape=jax.ShapeDtypeStruct((FL, ROWS, NLON), F32),
        in_specs=[whole()] * 2 + [smem] * 2 + [whole()] * 3,
        out_specs=whole(),
        scratch_shapes=[pltpu.VMEM((N1, 120, 256), F32), pltpu.VMEM((256, NM), F32)],
        compiler_params=parameters(),
        cost_estimate=cost(4e9, 8e6),
        name="inverse",
    )(rows, owner_column, lat_weights, place, twiddle, *backward)
    return out.reshape(3, 6, ROWS, NLON)


def solution(mesh):
    fine = Mesh(mesh.devices.reshape(2, 4, 2, 8), ("yh", "z", "core", "wave"))
    lat = ("yh", "z", "core")
    rows = P(None, None, lat + ("wave",), None)
    in_specs = (rows, P(), P("wave", lat, None), P(lat), P(), P(), P(), P(), P())
    return jax.shard_map(
        per_device, mesh=fine, in_specs=in_specs, out_specs=rows, check_vma=False
    )
```

```python
import math

import jax
import jax.numpy as jnp
import numpy as np
from jax import lax
from jax.experimental import pallas as pl
from jax.experimental.pallas import tpu as pltpu
from jax.sharding import Mesh, PartitionSpec as P

NLON = 2560
NM = 1280
PAIRS = 640
LAT = 640
PACK = 1408
FL = 18
ROWS = 5
N1 = 20
N2 = 128
HALF = 40
BF = jnp.bfloat16
F32 = jnp.float32
CHUNKS = ((0, 6), (6, 4))
UP = [(i, (i + 1) % 4) for i in range(4)]
DOWN = [(i, (i + 3) % 4) for i in range(4)]
SWAP = [(0, 1), (1, 0)]
VMEM_BYTES = 40 * 1024 * 1024


def split(x):
    high = x.astype(BF)
    return high, (x - high.astype(F32)).astype(BF)


def dot3(x, weight_high, weight_low, dims):
    high, low = split(x)
    out = lax.dot_general(high, weight_high, dims, preferred_element_type=F32)
    out += lax.dot_general(low, weight_high, dims, preferred_element_type=F32)
    return out + lax.dot_general(high, weight_low, dims, preferred_element_type=F32)


NN = (((1,), (0,)), ((), ()))
NT = (((1,), (1,)), ((), ()))


def constant_tables():
    scale = math.sqrt(2.0 / NLON)
    wave1 = np.arange(N1)[:, None]
    lon2 = np.arange(N2)[None, :]
    turn = 2.0 * np.pi * ((wave1 * lon2) % NLON) / NLON
    twiddle = np.stack([np.cos(turn), np.sin(turn)]).astype(np.float32)
    angle = 2.0 * np.pi * ((np.arange(N2)[:, None] * np.arange(64)[None, :]) % N2) / N2
    cos, sin = np.cos(angle) * scale, np.sin(angle) * scale
    zero = np.zeros_like(cos)
    forward = np.concatenate(
        [
            np.concatenate([cos, zero, -sin, zero], 1),
            np.concatenate([sin, zero, cos, zero], 1),
            np.concatenate([zero, cos, zero, -sin], 1),
            np.concatenate([zero, sin, zero, cos], 1),
        ],
        0,
    ).astype(np.float32)
    backward = np.concatenate(
        [
            np.concatenate([cos.T, sin.T, zero.T, zero.T], 1),
            np.concatenate([zero.T, zero.T, cos.T, sin.T], 1),
            np.concatenate([-sin.T, cos.T, zero.T, zero.T], 1),
            np.concatenate([zero.T, zero.T, -sin.T, cos.T], 1),
        ],
        0,
    ).astype(np.float32)

    def parts(table):
        high = table.astype(jnp.bfloat16)
        return high, (table - high.astype(np.float32)).astype(jnp.bfloat16)

    return twiddle, parts(forward), parts(backward)


def lane_waves():
    lane = lax.broadcasted_iota(jnp.int32, (1, NM), 1)
    return 2 * (lane // N2) + (lane % N2) // 64 + N1 * (lane % 64)


def one_hot(owner_ref, start, rows):
    column = owner_ref[start : start + rows, 0:1]
    waves = lane_waves()
    second = jnp.where(NM - 1 - column == waves, 1.0, 0.0).astype(BF)
    first = jnp.where(column == waves, 1.0, 0.0).astype(BF)
    return jnp.concatenate([second, first], axis=0)


def fourier_kernel(place_ref, grid_ref, owner_ref, twiddle_ref, high_ref, low_ref, table_ref, *refs):
    parts = len(CHUNKS)
    send_refs, away_refs = refs[:parts], refs[parts : 2 * parts]
    stage_ref, wide_ref, half_ref, sem = refs[2 * parts :]
    source = (1 - place_ref[0]) * HALF
    fetches, copies = [], []
    for k, (start, count) in enumerate(CHUNKS):
        for z in range(4):
            rows = pl.ds(4 * start + z * count, count)
            fetches.append(
                pltpu.make_async_copy(
                    table_ref.at[pl.ds(source + z * 10 + start, count)],
                    half_ref.at[rows],
                    sem.at[4 * k + z],
                )
            )
            fetches[-1].start()
            copies.append(
                pltpu.make_async_copy(
                    half_ref.at[rows],
                    away_refs[k].at[pl.ds(z * count, count)],
                    sem.at[4 * parts + 4 * k + z],
                )
            )
    for r in range(ROWS):
        tiles = [grid_ref[:, r, :, N2 * x1 : N2 * (x1 + 1)] for x1 in range(N1)]
        sums = [tiles[x1] + tiles[x1 + 10] for x1 in range(10)]
        differences = [tiles[x1] - tiles[x1 + 10] for x1 in range(10)]
        for m1 in range(11):
            source = sums if m1 % 2 == 0 else differences
            real, imag = source[0], None
            for x1 in range(1, 10):
                turn = 2.0 * math.pi * ((m1 * x1) % N1) / N1
                cos, sin = math.cos(turn), math.sin(turn)
                real = real + source[x1] * cos
                if m1 % 10:
                    term = source[x1] * (-sin)
                    imag = term if imag is None else imag + term
            if imag is None:
                imag = jnp.zeros_like(real)
            for wave, sign in ((m1, 1.0), (N1 - m1, -1.0)):
                if wave in (m1, N1) and sign < 0:
                    continue
                cos = twiddle_ref[0, wave : wave + 1, :]
                sin = twiddle_ref[1, wave : wave + 1, :]
                rotated_real = real * cos + (sign * imag) * sin
                rotated_imag = (sign * imag) * cos - real * sin
                base = (wave % 2) * 256
                rows = slice(3 * r, 3 * r + 3)
                stage_ref[wave // 2, rows, 0:6, base : base + N2] = rotated_real
                stage_ref[wave // 2, rows, 0:6, base + N2 : base + 256] = rotated_imag
    for fetch, copy in zip(fetches, copies):
        fetch.wait()
        copy.start()
    wide_ref[...] = jnp.zeros_like(wide_ref)
    for t in range(N1 // 2):
        out = dot3(stage_ref[t].reshape(120, 512), high_ref[...], low_ref[...], NN)
        for r in range(ROWS):
            rows = [out[r * 24 + f * 8 : r * 24 + f * 8 + 6] for f in range(3)]
            both = [row[:, :N2] for row in rows] + [row[:, N2:] for row in rows]
            both = jnp.concatenate(both, axis=0)
            wide_ref[r * 40 : r * 40 + 36, t * N2 : (t + 1) * N2] = both
    high, low = split(wide_ref[...])

    for k, (start, count) in enumerate(CHUNKS):
        group = 4 * count
        for c in range(2):
            picks = one_hot(owner_ref, 64 * start + c * 8 * group, 8 * group)
            out = lax.dot_general(picks, high, NT, preferred_element_type=F32)
            out += lax.dot_general(picks, low, NT, preferred_element_type=F32)
            for r in range(ROWS):
                lanes = out[:, r * 40 : (r + 1) * 40]
                half = 8 * group
                tile = [lanes[:half], lanes[half:], jnp.zeros((half, 48), F32)]
                tile = jnp.concatenate(tile, axis=1)
                for w in range(8):
                    send_refs[k][c * 8 + w, r] = tile[w * group : (w + 1) * group]
    for copy in copies:
        copy.wait()


def inverse_kernel(owner_ref, weight_ref, place_ref, twiddle_ref, high_ref, low_ref, *refs):
    got_refs = refs[: len(CHUNKS)]
    out_ref, stage_ref, wide_ref = refs[len(CHUNKS) :]
    wave = place_ref[1]

    fresh = True
    for k, (start, count) in enumerate(CHUNKS):
        group = 4 * count
        for c in range(2):
            picks = one_hot(owner_ref, 64 * start + c * 8 * group, 8 * group)
            seconds, firsts = [], []
            for r in range(ROWS):
                pieces = [got_refs[k][c * 8 + w, r] for w in range(8)]
                tile = jnp.concatenate(pieces, axis=0) * weight_ref[wave * ROWS + r]
                seconds.append(tile[:, 0:40])
                firsts.append(tile[:, 40:80])
            pad = [jnp.zeros((8 * group, 56), F32)]
            both = [jnp.concatenate(part + pad, axis=1) for part in (seconds, firsts)]
            high, low = split(jnp.concatenate(both, axis=0).T)
            out = lax.dot_general(high, picks, NN, preferred_element_type=F32)
            out += lax.dot_general(low, picks, NN, preferred_element_type=F32)
            if fresh:
                wide_ref[...] = out
            else:
                wide_ref[...] += out
            fresh = False
    for t in range(N1 // 2):
        rows = []
        for r in range(ROWS):
            block = wide_ref[r * 40 : (r + 1) * 40, t * N2 : (t + 1) * N2]
            gap = jnp.zeros((2, N2), F32)
            real, imag = [], []
            for f in range(3):
                real += [block[f * 6 : f * 6 + 6], gap]
                imag += [block[FL + f * 6 : FL + f * 6 + 6], gap]
            both = [jnp.concatenate(real, axis=0), jnp.concatenate(imag, axis=0)]
            rows.append(jnp.concatenate(both, axis=1))
        out = dot3(jnp.concatenate(rows, axis=0), high_ref[...], low_ref[...], NN)
        for odd in range(2):
            m1 = 2 * t + odd
            real = out[:, odd * 256 : odd * 256 + N2]
            imag = out[:, odd * 256 + N2 : odd * 256 + 256]
            cos = twiddle_ref[0, m1 : m1 + 1, :]
            sin = twiddle_ref[1, m1 : m1 + 1, :]
            stage_ref[m1, :, :N2] = real * cos - imag * sin
            stage_ref[m1, :, N2:] = real * sin + imag * cos
    for r in range(ROWS):
        rows = slice(r * 24, (r + 1) * 24)
        zero, ten = stage_ref[0, rows, :N2], stage_ref[10, rows, :N2]
        sums, gaps = [None], [None]
        for m in range(1, 10):
            sums.append(stage_ref[m, rows, :N2] + stage_ref[N1 - m, rows, :N2])
            gaps.append(stage_ref[m, rows, N2:] - stage_ref[N1 - m, rows, N2:])
        for x1 in range(10):
            even = zero + ten if x1 % 2 == 0 else zero - ten
            odd = jnp.zeros_like(zero)
            for m in range(1, 10):
                turn = 2.0 * math.pi * ((m * x1) % N1) / N1
                term = sums[m] * math.cos(turn) - gaps[m] * math.sin(turn)
                if m % 2 == 0:
                    even = even + term
                else:
                    odd = odd + term
            for f in range(3):
                rows6 = slice(f * 8, f * 8 + 6)
                out_ref[f, r, :, x1 * N2 : (x1 + 1) * N2] = (even + odd)[rows6]
                out_ref[f, r, :, (x1 + 10) * N2 : (x1 + 11) * N2] = (even - odd)[rows6]


def relative(rels, step):
    value = jnp.int32(rels[-1])
    for k, rel in enumerate(rels[:-1]):
        value = jnp.where(step == k, rel, value)
    return value


def spectra_kernel(start, count, rels, place_ref, owner_ref, own_ref, other_ref, four_ref, *refs):
    target, step = pl.program_id(0), pl.program_id(1)
    core, wave = place_ref[0], place_ref[1]
    z = lax.rem(place_ref[2] + relative(rels, target), 4)
    out_refs, work_ref = refs[:-1], refs[-1]
    extra = count * 36
    group = 4 * count
    side = 40 * group

    @pl.when(step == 0)
    def _():
        work_ref[extra : extra + 8, :] = jnp.zeros((8, NM), F32)

    lane = lax.broadcasted_iota(jnp.int32, (1, NM), 1)
    narrow = lax.broadcasted_iota(jnp.int32, (1, N2), 1)
    kept = []
    for i in range(2):
        first_wave = owner_ref[wave * 80 + core * HALF + z * 10 + start + 2 * step + i]
        pair = z * count + 2 * step + i
        mine = four_ref[pl.ds(core * side + pair, HALF, stride=group), :]
        theirs = four_ref[pl.ds((1 - core) * side + pair, HALF, stride=group), :]
        four = jnp.concatenate([mine, theirs], axis=0)
        four_high = four.astype(BF).astype(F32)
        left = jnp.concatenate([four_high, four_high, four - four_high], axis=0).T
        table = jnp.concatenate([own_ref[i], other_ref[i]], axis=0)
        main = table[:, :NM]
        main_high = main.astype(BF).astype(F32)
        right = jnp.concatenate([main_high, main - main_high, main_high], axis=0)
        both = lax.dot_general(left[:80].astype(BF), right.astype(BF), NN, preferred_element_type=F32)
        kept.append(jnp.where(lane < NM - first_wave, both[40:80], both[0:40])[:36])
        last = jnp.sum(table[:, NM : NM + 1] * four, axis=0, keepdims=True)
        spot = pl.multiple_of((2 * step + i) * N2, N2)
        work_ref[extra : extra + 1, pl.ds(spot, N2)] = jnp.where(narrow < 36, last, 0.0)
    work_ref[pl.ds(pl.multiple_of(step * 72, 8), 72), :] = jnp.concatenate(kept, axis=0)

    @pl.when(step == count // 2 - 1)
    def _():
        if len(rels) == 1:
            cut = halves(count)
            out_refs[0][...] = work_ref[:cut]
            out_refs[1][...] = work_ref[cut:]
        else:
            for k, out_ref in enumerate(out_refs):

                @pl.when(target == k)
                def _(out_ref=out_ref):
                    out_ref[...] = work_ref[...]


def halves(count):
    return (count * 36 + 8) // 16 * 8


def implicit_rows(load, degree, modes_e, modes_f, rates, height, heating):
    q = degree * (degree + 1.0) / float(NM * (NM + 1))
    rotation = 1.0 / (1.0 + 4.0 * q * q)
    damping = [1.0 / (1.0 + 4.0 * q * rates[i]) for i in range(6)]
    out = []
    for part in range(2):
        base = part * FL
        d = [load(base + 6 + l) for l in range(6)]
        t = [load(base + 12 + l) for l in range(6)]
        forced = []
        for l in range(6):
            total = d[l]
            for h in range(6):
                total = total - heating[h * 6 + l] * t[h]
            forced.append(total)
        modal = []
        for i in range(6):
            total = modes_e[i] * forced[0]
            for h in range(1, 6):
                total = total + modes_e[h * 6 + i] * forced[h]
            modal.append(total * damping[i])
        spread = []
        for l in range(6):
            total = modes_f[l] * modal[0]
            for i in range(1, 6):
                total = total + modes_f[i * 6 + l] * modal[i]
            spread.append(total)
        out += [load(base + l) * rotation for l in range(6)]
        out += spread
        for l in range(6):
            total = height[l] * spread[0]
            for h in range(1, 6):
                total = total + height[h * 6 + l] * spread[h]
            out.append(t[l] - q * total)
    return out


def implicit_kernel(start, count, place_ref, owner_ref, e_ref, f_ref, rate_ref, height_ref, heat_ref, x_ref, y_ref, out_ref):
    core, wave, z = place_ref[0], place_ref[1], place_ref[2]
    matrices = [[ref[i] for i in range(36)] for ref in (e_ref, f_ref)]
    rates = [rate_ref[i] for i in range(6)]
    heights = [[ref[i] for i in range(36)] for ref in (height_ref, heat_ref)]
    arguments = (matrices[0], matrices[1], rates, heights[0], heights[1])
    row = lax.broadcasted_iota(jnp.int32, (count, 1), 0)
    first_wave = jnp.zeros((count, 1), jnp.int32)
    for i in range(count):
        value = owner_ref[wave * 80 + core * HALF + z * 10 + start + i]
        first_wave = jnp.where(row == i, value, first_wave)

    tile = pl.program_id(0)
    packed = tile * N2 + lax.broadcasted_iota(jnp.int32, (count, N2), 1)
    degree = jnp.where(packed < NM - first_wave, first_wave + packed, packed - 1).astype(F32)

    def load(j):
        spot = pl.ds(j, count, stride=36)
        return x_ref[spot, :] + y_ref[spot, :]

    for j, value in enumerate(implicit_rows(load, degree, *arguments)):
        out_ref[pl.ds(j, count, stride=36), :] = value
    extra = count * 36
    line = x_ref[extra : extra + 1, :] + y_ref[extra : extra + 1, :]
    flipped = jnp.broadcast_to(line, (8, N2)).T
    degree = jnp.full((1, 8), NM - 1.0, F32)
    values = implicit_rows(lambda j: flipped[j : j + 1], degree, *arguments)
    values.append(jnp.zeros((N2 - 36, 8), F32))
    out_ref[extra : extra + 8, :] = jnp.concatenate(values, axis=0).T


def grid_rows_kernel(start, count, rels, place_ref, owner_ref, own_ref, other_ref, *refs):
    target, step = pl.program_id(0), pl.program_id(1)
    core, wave = place_ref[0], place_ref[1]
    z = lax.rem(place_ref[2] + relative(rels, target), 4)
    spec_refs, (out_ref, work_ref) = refs[:-2], refs[-2:]
    extra = count * 36
    group = 4 * count
    side = 40 * group
    cut = halves(count)

    for k in range(4):

        @pl.when((target == k) & (step == 0))
        def _(k=k):
            if k < 3:
                work_ref[...] = spec_refs[k][...]
            else:
                work_ref[:cut] = spec_refs[3][...]
                work_ref[cut:] = spec_refs[4][...]

    lane = lax.broadcasted_iota(jnp.int32, (1, NM), 1)
    block = work_ref[pl.ds(pl.multiple_of(step * 72, 8), 72), :]
    pad = jnp.zeros((4, NM), F32)
    for i in range(2):
        first_wave = owner_ref[wave * 80 + core * HALF + z * 10 + start + 2 * step + i]
        pair = z * count + 2 * step + i
        values = jnp.concatenate([block[i * 36 : i * 36 + 36], pad], axis=0)
        is_first = lane < NM - first_wave
        both = jnp.concatenate(
            [jnp.where(is_first, 0.0, values), jnp.where(is_first, values, 0.0)], axis=0
        )
        high, low = split(both)
        table = jnp.concatenate([own_ref[i], other_ref[i]], axis=0)
        back = dot3(table[:, :NM], high, low, NT)
        back = jnp.concatenate([back, jnp.zeros((80, 48), F32)], axis=1)
        spot = pl.multiple_of((2 * step + i) * N2, N2)
        last = work_ref[extra : extra + 1, pl.ds(spot, N2)]
        back = back + table[:, NM : NM + 1] * last
        out_ref[pl.ds(core * side + pair, HALF, stride=group), :] = back[:HALF]
        out_ref[pl.ds((1 - core) * side + pair, HALF, stride=group), :] = back[HALF:]


def parameters():
    return pltpu.CompilerParams(vmem_limit_bytes=VMEM_BYTES)


def whole(space=pltpu.VMEM):
    return pl.BlockSpec(memory_space=space)


def cost(flops, size):
    return pl.CostEstimate(flops=int(flops), bytes_accessed=int(size), transcendentals=0)


def per_device(
    grad_grid, owner, legendre, lat_weights, modes_e, modes_f, rates, height_matrix, heating_matrix
):
    core, wave, z = lax.axis_index("core"), lax.axis_index("wave"), lax.axis_index("z")
    twiddle, forward, backward = constant_tables()
    smem = whole(pltpu.SMEM)
    place = jnp.stack([core, wave, z]).astype(jnp.int32)
    by_group = owner.reshape(8, 2, 4, 10)
    order = [by_group[..., a : a + n].transpose(1, 0, 2, 3).reshape(-1) for a, n in CHUNKS]
    owner_column = jnp.broadcast_to(jnp.concatenate(order)[:, None], (PAIRS, N2))
    matrices = [m.reshape(36) for m in (modes_e, modes_f)] + [rates]
    matrices += [m.reshape(36) for m in (height_matrix, heating_matrix)]

    made = pl.pallas_call(
        fourier_kernel,
        out_shape=[jax.ShapeDtypeStruct((16, ROWS, 4 * n, N2), F32) for _, n in CHUNKS]
        + [jax.ShapeDtypeStruct((4 * n, HALF, PACK), F32) for _, n in CHUNKS],
        in_specs=[smem] + [whole()] * 5 + [whole(pl.ANY)],
        out_specs=[whole()] * len(CHUNKS) + [whole(pl.ANY)] * len(CHUNKS),
        scratch_shapes=[
            pltpu.VMEM((10, 15, 8, 512), F32),
            pltpu.VMEM((208, NM), F32),
            pltpu.VMEM((HALF, HALF, PACK), F32),
            pltpu.SemaphoreType.DMA((8 * len(CHUNKS),)),
        ],
        compiler_params=parameters(),
        cost_estimate=cost(4e9, 2.6e7),
        name="fourier",
    )(place, grad_grid.transpose(0, 2, 1, 3), owner_column, twiddle, *forward, legendre)
    fours, aways = made[: len(CHUNKS)], made[len(CHUNKS) :]

    def zone(rels, t, place):
        return lax.rem(place[2] + relative(rels, t), 4)

    def table_specs(start, count, rels):
        return [
            pl.BlockSpec(
                (2, HALF, PACK),
                lambda t, s, place, owner: (
                    place[0] * 20 + zone(rels, t, place) * 5 + start // 2 + s,
                    0,
                    0,
                ),
            ),
            pl.BlockSpec(
                (2, HALF, PACK),
                lambda t, s, place, owner: (zone(rels, t, place) * (count // 2) + s, 0, 0),
            ),
        ]

    def kept(rows, lanes):
        return pl.BlockSpec((rows, lanes), lambda t, s, place, owner: (0, 0))

    def spectra(start, count, rels, four, other):
        height = count * 36 + 8
        cut = halves(count)
        rows = [cut, height - cut] if len(rels) == 1 else [height] * len(rels)
        return pl.pallas_call(
            lambda *refs: spectra_kernel(start, count, rels, *refs),
            out_shape=[jax.ShapeDtypeStruct((n, NM), F32) for n in rows],
            grid_spec=pltpu.PrefetchScalarGridSpec(
                num_scalar_prefetch=2,
                grid=(len(rels), count // 2),
                in_specs=table_specs(start, count, rels) + [kept(320 * count, N2)],
                out_specs=[kept(n, NM) for n in rows],
                scratch_shapes=[pltpu.VMEM((height, NM), F32)],
            ),
            compiler_params=parameters(),
            cost_estimate=cost(5e7 * count * len(rels), 5e5 * count * len(rels)),
            name="spectra",
        )(place, owner, legendre, other, four)

    def implicit(start, count, mine, theirs):
        height = count * 36 + 8
        return pl.pallas_call(
            lambda *refs: implicit_kernel(start, count, *refs),
            out_shape=jax.ShapeDtypeStruct((height, NM), F32),
            grid=(10,),
            in_specs=[smem] * 7 + [pl.BlockSpec((height, N2), lambda t: (0, t))] * 2,
            out_specs=pl.BlockSpec((height, N2), lambda t: (0, t)),
            compiler_params=parameters(),
            cost_estimate=cost(1e7 * count, 6e5 * count),
            name="implicit",
        )(place, owner, *matrices, mine, theirs)

    def grid_rows(start, count, other, blocks):
        height = count * 36 + 8
        cut = halves(count)
        rels = (0, 1, 3, 2)
        rows = pl.pallas_call(
            lambda *refs: grid_rows_kernel(start, count, rels, *refs),
            out_shape=jax.ShapeDtypeStruct((320 * count, N2), F32),
            grid_spec=pltpu.PrefetchScalarGridSpec(
                num_scalar_prefetch=2,
                grid=(4, count // 2),
                in_specs=table_specs(start, count, rels)
                + [kept(n, NM) for n in (height, height, height, cut, height - cut)],
                out_specs=kept(320 * count, N2),
                scratch_shapes=[pltpu.VMEM((height, NM), F32)],
            ),
            compiler_params=parameters(),
            cost_estimate=cost(3e8 * count, 2e6 * count),
            name="grid_rows",
        )(place, owner, legendre, other, *blocks)
        return rows.reshape(16, ROWS, 4 * count, N2)

    def after(value, *earlier):
        return lax.optimization_barrier((value,) + earlier)[0]

    def exchange(value):
        return lax.all_to_all(value, ("core", "wave"), 0, 0, tiled=True)

    steps = [{} for _ in CHUNKS]
    for k, (start, count) in enumerate(CHUNKS):
        now, before = steps[k], steps[k - 1] if k else None
        now["cut"] = cut = halves(count)
        now["other"] = lax.ppermute(aways[k], "core", SWAP)
        four = fours[k] if k == 0 else after(fours[k], before["opposite"][0])
        four = exchange(four).reshape(320 * count, N2)
        if k:
            four = after(four, before["right"], before["left"])
        now["opposite"] = top, bottom = spectra(start, count, (2,), four, now["other"])
        top = lax.ppermute(top, "z", UP)
        bottom = lax.ppermute(bottom, "z", DOWN)
        right, left, mine = spectra(start, count, (1, 3, 0), four, now["other"])
        if k:
            top = after(top, before["sum"])
        now["right"] = right = right.at[:cut].add(top)
        now["left"] = left = left.at[cut:].add(bottom)
        now["sum"] = mine + lax.ppermute(right, "z", UP) + lax.ppermute(left, "z", DOWN)
        now["theirs"] = lax.ppermute(now["sum"], "yh", SWAP)
    for k, (start, count) in enumerate(CHUNKS):
        now, before = steps[k], steps[k - 1] if k else None
        theirs = after(now["theirs"], *before["ends"]) if k else now["theirs"]
        now["new"] = new = implicit(start, count, now["sum"], theirs)
        left = lax.ppermute(new, "z", UP)
        right = lax.ppermute(new, "z", DOWN)
        now["left"], now["right"] = left, right
        now["ends"] = left[: now["cut"]], right[now["cut"] :]
        now["top"] = lax.ppermute(now["ends"][0], "z", UP)
        now["bottom"] = lax.ppermute(now["ends"][1], "z", DOWN)
    results = []
    for k, (start, count) in enumerate(CHUNKS):
        now = steps[k]
        top = now["top"]
        if k + 1 < len(CHUNKS):
            top = after(top, steps[k + 1]["new"])
        blocks = (now["new"], now["right"], now["left"], top, now["bottom"])
        results.append(exchange(grid_rows(start, count, now["other"], blocks)))
    out = pl.pallas_call(
        inverse_kernel,
        out_shape=jax.ShapeDtypeStruct((3, ROWS, 6, NLON), F32),
        in_specs=[whole()] + [smem] * 2 + [whole()] * (3 + len(CHUNKS)),
        out_specs=whole(),
        scratch_shapes=[pltpu.VMEM((N1, 120, 256), F32), pltpu.VMEM((256, NM), F32)],
        compiler_params=parameters(),
        cost_estimate=cost(4e9, 8e6),
        name="inverse",
    )(owner_column, lat_weights, place, twiddle, *backward, *results)
    return out.transpose(0, 2, 1, 3)


def solution(mesh):
    fine = Mesh(mesh.devices.reshape(2, 4, 2, 8), ("yh", "z", "core", "wave"))
    lat = ("yh", "z", "core")
    rows = P(None, None, lat + ("wave",), None)
    in_specs = (rows, P(), P("wave", lat, None), P(lat), P(), P(), P(), P(), P())
    return jax.shard_map(
        per_device, mesh=fine, in_specs=in_specs, out_specs=rows, check_vma=False
    )
```

```python
import math

import jax
import jax.numpy as jnp
import numpy as np
from jax import lax
from jax.experimental import pallas as pl
from jax.experimental.pallas import tpu as pltpu
from jax.sharding import Mesh, PartitionSpec as P

NLON = 2560
NM = 1280
PAIRS = 640
LAT = 640
PACK = 1408
FL = 18
ROWS = 5
N1 = 20
N2 = 128
HALF = 40
BF = jnp.bfloat16
F32 = jnp.float32
CHUNKS = ((0, 6), (6, 4))
UP = [(i, (i + 1) % 4) for i in range(4)]
DOWN = [(i, (i + 3) % 4) for i in range(4)]
SWAP = [(0, 1), (1, 0)]
VMEM_BYTES = 40 * 1024 * 1024


def split(x):
    high = x.astype(BF)
    return high, (x - high.astype(F32)).astype(BF)


def dot3(x, weight_high, weight_low, dims):
    high, low = split(x)
    out = lax.dot_general(high, weight_high, dims, preferred_element_type=F32)
    out += lax.dot_general(low, weight_high, dims, preferred_element_type=F32)
    return out + lax.dot_general(high, weight_low, dims, preferred_element_type=F32)


NN = (((1,), (0,)), ((), ()))
NT = (((1,), (1,)), ((), ()))


def constant_tables():
    scale = math.sqrt(2.0 / NLON)
    wave1 = np.arange(N1)[:, None]
    lon2 = np.arange(N2)[None, :]
    turn = 2.0 * np.pi * ((wave1 * lon2) % NLON) / NLON
    twiddle = np.stack([np.cos(turn), np.sin(turn)]).astype(np.float32)
    angle = 2.0 * np.pi * ((np.arange(N2)[:, None] * np.arange(64)[None, :]) % N2) / N2
    cos, sin = np.cos(angle) * scale, np.sin(angle) * scale
    zero = np.zeros_like(cos)
    forward = np.concatenate(
        [
            np.concatenate([cos, zero, -sin, zero], 1),
            np.concatenate([sin, zero, cos, zero], 1),
            np.concatenate([zero, cos, zero, -sin], 1),
            np.concatenate([zero, sin, zero, cos], 1),
        ],
        0,
    ).astype(np.float32)
    backward = np.concatenate(
        [
            np.concatenate([cos.T, sin.T, zero.T, zero.T], 1),
            np.concatenate([zero.T, zero.T, cos.T, sin.T], 1),
            np.concatenate([-sin.T, cos.T, zero.T, zero.T], 1),
            np.concatenate([zero.T, zero.T, -sin.T, cos.T], 1),
        ],
        0,
    ).astype(np.float32)

    def parts(table):
        high = table.astype(jnp.bfloat16)
        return high, (table - high.astype(np.float32)).astype(jnp.bfloat16)

    return twiddle, parts(forward), parts(backward)


def lane_waves():
    lane = lax.broadcasted_iota(jnp.int32, (1, NM), 1)
    return 2 * (lane // N2) + (lane % N2) // 64 + N1 * (lane % 64)


def one_hot(owner_ref, start, rows):
    column = owner_ref[start : start + rows, 0:1]
    waves = lane_waves()
    second = jnp.where(NM - 1 - column == waves, 1.0, 0.0).astype(BF)
    first = jnp.where(column == waves, 1.0, 0.0).astype(BF)
    return second, first


def fourier_kernel(place_ref, owner_ref, *refs):
    parts = len(CHUNKS)
    sources, table_ref, refs = refs[:4], refs[4], refs[5:]
    send_refs, away_refs = refs[:parts], refs[parts : 2 * parts]
    stage_ref, wide_ref, half_ref, sem = refs[2 * parts : 2 * parts + 4]
    locals_ = refs[2 * parts + 4 :]
    grid_ref, twiddle_ref, high_ref, low_ref = locals_
    loads = []
    for k in range(4):
        loads.append(pltpu.make_async_copy(sources[k], locals_[k], sem.at[8 * parts + k]))
        loads[-1].start()
    source = (1 - place_ref[0]) * HALF
    fetches, copies = [], []
    for k, (start, count) in enumerate(CHUNKS):
        for z in range(4):
            rows = pl.ds(4 * start + z * count, count)
            fetches.append(
                pltpu.make_async_copy(
                    table_ref.at[pl.ds(source + z * 10 + start, count)],
                    half_ref.at[rows],
                    sem.at[4 * k + z],
                )
            )
            fetches[-1].start()
            copies.append(
                pltpu.make_async_copy(
                    half_ref.at[rows],
                    away_refs[k].at[pl.ds(z * count, count)],
                    sem.at[4 * parts + 4 * k + z],
                )
            )
    loads[0].wait()
    loads[1].wait()
    for r in range(ROWS):
        tiles = [grid_ref[:, r, :, N2 * x1 : N2 * (x1 + 1)] for x1 in range(N1)]
        sums = [tiles[x1] + tiles[x1 + 10] for x1 in range(10)]
        differences = [tiles[x1] - tiles[x1 + 10] for x1 in range(10)]
        for m1 in range(11):
            source = sums if m1 % 2 == 0 else differences
            real, imag = source[0], None
            for x1 in range(1, 10):
                turn = 2.0 * math.pi * ((m1 * x1) % N1) / N1
                cos, sin = math.cos(turn), math.sin(turn)
                real = real + source[x1] * cos
                if m1 % 10:
                    term = source[x1] * (-sin)
                    imag = term if imag is None else imag + term
            if imag is None:
                imag = jnp.zeros_like(real)
            for wave, sign in ((m1, 1.0), (N1 - m1, -1.0)):
                if wave in (m1, N1) and sign < 0:
                    continue
                cos = twiddle_ref[0, wave : wave + 1, :]
                sin = twiddle_ref[1, wave : wave + 1, :]
                rotated_real = real * cos + (sign * imag) * sin
                rotated_imag = (sign * imag) * cos - real * sin
                base = (wave % 2) * 256
                rows = slice(3 * r, 3 * r + 3)
                stage_ref[wave // 2, rows, 0:6, base : base + N2] = rotated_real
                stage_ref[wave // 2, rows, 0:6, base + N2 : base + 256] = rotated_imag
    loads[2].wait()
    loads[3].wait()
    for fetch, copy in zip(fetches, copies):
        fetch.wait()
        copy.start()
    wide_ref[...] = jnp.zeros_like(wide_ref)
    for t in range(N1 // 2):
        out = dot3(stage_ref[t].reshape(120, 512), high_ref[...], low_ref[...], NN)
        for r in range(ROWS):
            rows = [out[r * 24 + f * 8 : r * 24 + f * 8 + 6] for f in range(3)]
            both = [row[:, :N2] for row in rows] + [row[:, N2:] for row in rows]
            both = jnp.concatenate(both, axis=0)
            wide_ref[r * 36 : r * 36 + 36, t * N2 : (t + 1) * N2] = both
    high, low = split(wide_ref[...])

    for k, (start, count) in enumerate(CHUNKS):
        group = 4 * count
        for c in range(2):
            half = 8 * group
            picks = jnp.concatenate(one_hot(owner_ref, 64 * start + c * half, half), axis=0)
            out = lax.dot_general(picks, high, NT, preferred_element_type=F32)
            out += lax.dot_general(picks, low, NT, preferred_element_type=F32)
            tile = [out[:half, :180], out[half:, :180], jnp.zeros((half, 24), F32)]
            tile = jnp.concatenate(tile, axis=1)
            for w in range(8):
                for t in range(3):
                    rows = slice(w * group, (w + 1) * group)
                    send_refs[k][c * 8 + w, t] = tile[rows, t * N2 : (t + 1) * N2]
    for copy in copies:
        copy.wait()


def inverse_kernel(owner_ref, weight_ref, place_ref, twiddle_ref, high_ref, low_ref, *refs):
    got_refs = refs[: len(CHUNKS)]
    out_ref, stage_ref, wide_ref = refs[len(CHUNKS) :]
    wave = place_ref[1]

    fresh = True
    for k, (start, count) in enumerate(CHUNKS):
        group = 4 * count
        for c in range(2):
            half = 8 * group
            second, first = one_hot(owner_ref, 64 * start + c * half, half)
            tiles = [
                jnp.concatenate([got_refs[k][c * 8 + w, t] for w in range(8)], axis=0)
                for t in range(3)
            ]
            flipped = jnp.concatenate(tiles, axis=1).T
            out = jnp.zeros((184, NM), F32)
            for rows, picks in ((flipped[0:184], second), (flipped[180:364], first)):
                high, low = split(rows)
                out += lax.dot_general(high, picks, NN, preferred_element_type=F32)
                out += lax.dot_general(low, picks, NN, preferred_element_type=F32)
            if fresh:
                wide_ref[...] = out
            else:
                wide_ref[...] += out
            fresh = False
    for t in range(N1 // 2):
        rows = []
        for r in range(ROWS):
            block = wide_ref[r * 36 : (r + 1) * 36, t * N2 : (t + 1) * N2]
            block = block * weight_ref[wave * ROWS + r]
            gap = jnp.zeros((2, N2), F32)
            real, imag = [], []
            for f in range(3):
                real += [block[f * 6 : f * 6 + 6], gap]
                imag += [block[FL + f * 6 : FL + f * 6 + 6], gap]
            both = [jnp.concatenate(real, axis=0), jnp.concatenate(imag, axis=0)]
            rows.append(jnp.concatenate(both, axis=1))
        out = dot3(jnp.concatenate(rows, axis=0), high_ref[...], low_ref[...], NN)
        for odd in range(2):
            m1 = 2 * t + odd
            real = out[:, odd * 256 : odd * 256 + N2]
            imag = out[:, odd * 256 + N2 : odd * 256 + 256]
            cos = twiddle_ref[0, m1 : m1 + 1, :]
            sin = twiddle_ref[1, m1 : m1 + 1, :]
            stage_ref[m1, :, :N2] = real * cos - imag * sin
            stage_ref[m1, :, N2:] = real * sin + imag * cos
    for r in range(ROWS):
        rows = slice(r * 24, (r + 1) * 24)
        zero, ten = stage_ref[0, rows, :N2], stage_ref[10, rows, :N2]
        sums, gaps = [None], [None]
        for m in range(1, 10):
            sums.append(stage_ref[m, rows, :N2] + stage_ref[N1 - m, rows, :N2])
            gaps.append(stage_ref[m, rows, N2:] - stage_ref[N1 - m, rows, N2:])
        for x1 in range(10):
            even = zero + ten if x1 % 2 == 0 else zero - ten
            odd = jnp.zeros_like(zero)
            for m in range(1, 10):
                turn = 2.0 * math.pi * ((m * x1) % N1) / N1
                term = sums[m] * math.cos(turn) - gaps[m] * math.sin(turn)
                if m % 2 == 0:
                    even = even + term
                else:
                    odd = odd + term
            for f in range(3):
                rows6 = slice(f * 8, f * 8 + 6)
                out_ref[f, r, :, x1 * N2 : (x1 + 1) * N2] = (even + odd)[rows6]
                out_ref[f, r, :, (x1 + 10) * N2 : (x1 + 11) * N2] = (even - odd)[rows6]


def relative(rels, step):
    value = jnp.int32(rels[-1])
    for k, rel in enumerate(rels[:-1]):
        value = jnp.where(step == k, rel, value)
    return value


def spectra_kernel(start, count, rels, place_ref, owner_ref, own_ref, other_ref, four_ref, *refs):
    target, step = pl.program_id(0), pl.program_id(1)
    core, wave = place_ref[0], place_ref[1]
    z = lax.rem(place_ref[2] + relative(rels, target), 4)
    out_refs, work_ref, four_work = refs[:-2], refs[-2], refs[-1]
    extra = count * 36
    group = 4 * count

    @pl.when(step == 0)
    def _():
        work_ref[extra : extra + 8, :] = jnp.zeros((8, NM), F32)

    lane = lax.broadcasted_iota(jnp.int32, (1, NM), 1)
    narrow = lax.broadcasted_iota(jnp.int32, (1, N2), 1)
    kept = []
    for i in range(2):
        first_wave = owner_ref[wave * 80 + core * HALF + z * 10 + start + 2 * step + i]
        pair = z * count + 2 * step + i
        for b, band in enumerate((core, 1 - core)):
            base = band * (24 * group) + pair
            tiles = [
                four_ref[pl.ds(base + t * group, 8, stride=3 * group), :] for t in range(3)
            ]
            line = jnp.concatenate(tiles, axis=1)
            for r in range(ROWS):
                pieces = [line[:, r * 36 : r * 36 + 36], jnp.zeros((8, 4), F32)]
                pieces += [line[:, 180 + r * 36 : 216 + r * 36], jnp.zeros((8, 52), F32)]
                piece = jnp.concatenate(pieces, axis=1)
                four_work[pl.ds(i * 80 + b * HALF + r, 8, stride=ROWS), :] = piece
        four = four_work[i * 80 : (i + 1) * 80, :]
        four_high = four.astype(BF).astype(F32)
        left = jnp.concatenate([four_high, four_high, four - four_high], axis=0).T
        table = jnp.concatenate([own_ref[i], other_ref[i]], axis=0)
        main = table[:, :NM]
        main_high = main.astype(BF).astype(F32)
        right = jnp.concatenate([main_high, main - main_high, main_high], axis=0)
        both = lax.dot_general(left[:80].astype(BF), right.astype(BF), NN, preferred_element_type=F32)
        kept.append(jnp.where(lane < NM - first_wave, both[40:80], both[0:40])[:36])
        last = jnp.sum(table[:, NM : NM + 1] * four, axis=0, keepdims=True)
        spot = pl.multiple_of((2 * step + i) * N2, N2)
        work_ref[extra : extra + 1, pl.ds(spot, N2)] = jnp.where(narrow < 36, last, 0.0)
    work_ref[pl.ds(pl.multiple_of(step * 72, 8), 72), :] = jnp.concatenate(kept, axis=0)

    @pl.when(step == count // 2 - 1)
    def _():
        if len(rels) == 1:
            cut = halves(count)
            out_refs[0][...] = work_ref[:cut]
            out_refs[1][...] = work_ref[cut:]
        else:
            for k, out_ref in enumerate(out_refs):

                @pl.when(target == k)
                def _(out_ref=out_ref):
                    out_ref[...] = work_ref[...]


def halves(count):
    return (count * 36 + 8) // 16 * 8


def implicit_rows(load, degree, modes_e, modes_f, rates, height, heating):
    q = degree * (degree + 1.0) / float(NM * (NM + 1))
    rotation = 1.0 / (1.0 + 4.0 * q * q)
    damping = [1.0 / (1.0 + 4.0 * q * rates[i]) for i in range(6)]
    out = []
    for part in range(2):
        base = part * FL
        d = [load(base + 6 + l) for l in range(6)]
        t = [load(base + 12 + l) for l in range(6)]
        forced = []
        for l in range(6):
            total = d[l]
            for h in range(6):
                total = total - heating[h * 6 + l] * t[h]
            forced.append(total)
        modal = []
        for i in range(6):
            total = modes_e[i] * forced[0]
            for h in range(1, 6):
                total = total + modes_e[h * 6 + i] * forced[h]
            modal.append(total * damping[i])
        spread = []
        for l in range(6):
            total = modes_f[l] * modal[0]
            for i in range(1, 6):
                total = total + modes_f[i * 6 + l] * modal[i]
            spread.append(total)
        out += [load(base + l) * rotation for l in range(6)]
        out += spread
        for l in range(6):
            total = height[l] * spread[0]
            for h in range(1, 6):
                total = total + height[h * 6 + l] * spread[h]
            out.append(t[l] - q * total)
    return out


def implicit_kernel(start, count, place_ref, owner_ref, e_ref, f_ref, rate_ref, height_ref, heat_ref, x_ref, y_ref, out_ref):
    core, wave, z = place_ref[0], place_ref[1], place_ref[2]
    matrices = [[ref[i] for i in range(36)] for ref in (e_ref, f_ref)]
    rates = [rate_ref[i] for i in range(6)]
    heights = [[ref[i] for i in range(36)] for ref in (height_ref, heat_ref)]
    arguments = (matrices[0], matrices[1], rates, heights[0], heights[1])
    row = lax.broadcasted_iota(jnp.int32, (count, 1), 0)
    first_wave = jnp.zeros((count, 1), jnp.int32)
    for i in range(count):
        value = owner_ref[wave * 80 + core * HALF + z * 10 + start + i]
        first_wave = jnp.where(row == i, value, first_wave)

    tile = pl.program_id(0)
    packed = tile * N2 + lax.broadcasted_iota(jnp.int32, (count, N2), 1)
    degree = jnp.where(packed < NM - first_wave, first_wave + packed, packed - 1).astype(F32)

    def load(j):
        spot = pl.ds(j, count, stride=36)
        return x_ref[spot, :] + y_ref[spot, :]

    for j, value in enumerate(implicit_rows(load, degree, *arguments)):
        out_ref[pl.ds(j, count, stride=36), :] = value
    extra = count * 36
    line = x_ref[extra : extra + 1, :] + y_ref[extra : extra + 1, :]
    flipped = jnp.broadcast_to(line, (8, N2)).T
    degree = jnp.full((1, 8), NM - 1.0, F32)
    values = implicit_rows(lambda j: flipped[j : j + 1], degree, *arguments)
    values.append(jnp.zeros((N2 - 36, 8), F32))
    out_ref[extra : extra + 8, :] = jnp.concatenate(values, axis=0).T


def grid_rows_kernel(start, count, rels, place_ref, owner_ref, own_ref, other_ref, *refs):
    target, step = pl.program_id(0), pl.program_id(1)
    core, wave = place_ref[0], place_ref[1]
    z = lax.rem(place_ref[2] + relative(rels, target), 4)
    out_ref, work_ref, back_work = refs[-3:]
    if len(rels) == 1:
        top_ref, bottom_ref, before_ref = refs[:-3]
    else:
        spec_refs = refs[:-3]
    extra = count * 36
    group = 4 * count
    cut = halves(count)

    for k in range(len(rels)):

        @pl.when((target == k) & (step == 0))
        def _(k=k):
            if len(rels) == 1:
                work_ref[:cut] = top_ref[...]
                work_ref[cut:] = bottom_ref[...]
                out_ref[...] = before_ref[...]
            else:
                work_ref[...] = spec_refs[k][...]

    lane = lax.broadcasted_iota(jnp.int32, (1, NM), 1)
    block = work_ref[pl.ds(pl.multiple_of(step * 72, 8), 72), :]
    pad = jnp.zeros((4, NM), F32)
    for i in range(2):
        first_wave = owner_ref[wave * 80 + core * HALF + z * 10 + start + 2 * step + i]
        pair = z * count + 2 * step + i
        values = jnp.concatenate([block[i * 36 : i * 36 + 36], pad], axis=0)
        is_first = lane < NM - first_wave
        both = jnp.concatenate(
            [jnp.where(is_first, 0.0, values), jnp.where(is_first, values, 0.0)], axis=0
        )
        high, low = split(both)
        table = jnp.concatenate([own_ref[i], other_ref[i]], axis=0)
        back = dot3(table[:, :NM], high, low, NT)
        back = jnp.concatenate([back, jnp.zeros((80, 48), F32)], axis=1)
        spot = pl.multiple_of((2 * step + i) * N2, N2)
        last = work_ref[extra : extra + 1, pl.ds(spot, N2)]
        back = back + table[:, NM : NM + 1] * last
        back_work[i * 80 : (i + 1) * 80, :] = back
        for b, band in enumerate((core, 1 - core)):
            rows = [
                back_work[pl.ds(i * 80 + b * HALF + r, 8, stride=ROWS), :] for r in range(ROWS)
            ]
            line = [row[:, 0:36] for row in rows] + [row[:, 40:76] for row in rows]
            line = jnp.concatenate(line + [jnp.zeros((8, 24), F32)], axis=1)
            base = band * (24 * group) + pair
            for t in range(3):
                spot = pl.ds(base + t * group, 8, stride=3 * group)
                out_ref[spot, :] = line[:, t * N2 : (t + 1) * N2]


def parameters():
    return pltpu.CompilerParams(vmem_limit_bytes=VMEM_BYTES)


def whole(space=pltpu.VMEM):
    return pl.BlockSpec(memory_space=space)


def cost(flops, size):
    return pl.CostEstimate(flops=int(flops), bytes_accessed=int(size), transcendentals=0)


def per_device(
    grad_grid, owner, legendre, lat_weights, modes_e, modes_f, rates, height_matrix, heating_matrix
):
    core, wave, z = lax.axis_index("core"), lax.axis_index("wave"), lax.axis_index("z")
    twiddle, forward, backward = constant_tables()
    smem = whole(pltpu.SMEM)
    place = jnp.stack([core, wave, z]).astype(jnp.int32)
    by_group = owner.reshape(8, 2, 4, 10)
    order = [by_group[..., a : a + n].transpose(1, 0, 2, 3).reshape(-1) for a, n in CHUNKS]
    owner_column = jnp.broadcast_to(jnp.concatenate(order)[:, None], (PAIRS, N2))
    matrices = [m.reshape(36) for m in (modes_e, modes_f)] + [rates]
    matrices += [m.reshape(36) for m in (height_matrix, heating_matrix)]

    made = pl.pallas_call(
        fourier_kernel,
        out_shape=[jax.ShapeDtypeStruct((16, 3, 4 * n, N2), F32) for _, n in CHUNKS]
        + [jax.ShapeDtypeStruct((4 * n, HALF, PACK), F32) for _, n in CHUNKS],
        in_specs=[smem, whole()] + [whole(pltpu.HBM)] * 5,
        out_specs=[whole()] * len(CHUNKS) + [whole(pltpu.HBM)] * len(CHUNKS),
        scratch_shapes=[
            pltpu.VMEM((10, 15, 8, 512), F32),
            pltpu.VMEM((184, NM), F32),
            pltpu.VMEM((HALF, HALF, PACK), F32),
            pltpu.SemaphoreType.DMA((8 * len(CHUNKS) + 4,)),
            pltpu.VMEM((3, ROWS, 6, NLON), F32),
            pltpu.VMEM((2, N1, N2), F32),
            pltpu.VMEM((512, 256), BF),
            pltpu.VMEM((512, 256), BF),
        ],
        compiler_params=parameters(),
        cost_estimate=cost(4e9, 2.6e7),
        name="fourier",
    )(place, owner_column, grad_grid.transpose(0, 2, 1, 3), twiddle, *forward, legendre)
    fours, aways = made[: len(CHUNKS)], made[len(CHUNKS) :]

    def zone(rels, t, place):
        return lax.rem(place[2] + relative(rels, t), 4)

    def table_specs(start, count, rels):
        return [
            pl.BlockSpec(
                (2, HALF, PACK),
                lambda t, s, place, owner: (
                    place[0] * 20 + zone(rels, t, place) * 5 + start // 2 + s,
                    0,
                    0,
                ),
            ),
            pl.BlockSpec(
                (2, HALF, PACK),
                lambda t, s, place, owner: (zone(rels, t, place) * (count // 2) + s, 0, 0),
            ),
        ]

    def kept(rows, lanes):
        return pl.BlockSpec((rows, lanes), lambda t, s, place, owner: (0, 0))

    def spectra(start, count, rels, four, other):
        height = count * 36 + 8
        cut = halves(count)
        rows = [cut, height - cut] if len(rels) == 1 else [height] * len(rels)
        return pl.pallas_call(
            lambda *refs: spectra_kernel(start, count, rels, *refs),
            out_shape=[jax.ShapeDtypeStruct((n, NM), F32) for n in rows],
            grid_spec=pltpu.PrefetchScalarGridSpec(
                num_scalar_prefetch=2,
                grid=(len(rels), count // 2),
                in_specs=table_specs(start, count, rels) + [kept(192 * count, N2)],
                out_specs=[kept(n, NM) for n in rows],
                scratch_shapes=[pltpu.VMEM((height, NM), F32), pltpu.VMEM((160, N2), F32)],
            ),
            compiler_params=parameters(),
            cost_estimate=cost(5e7 * count * len(rels), 5e5 * count * len(rels)),
            name="spectra",
        )(place, owner, legendre, other, four)

    def implicit(start, count, mine, theirs):
        height = count * 36 + 8
        return pl.pallas_call(
            lambda *refs: implicit_kernel(start, count, *refs),
            out_shape=jax.ShapeDtypeStruct((height, NM), F32),
            grid=(10,),
            in_specs=[smem] * 7 + [pl.BlockSpec((height, N2), lambda t: (0, t))] * 2,
            out_specs=pl.BlockSpec((height, N2), lambda t: (0, t)),
            compiler_params=parameters(),
            cost_estimate=cost(1e7 * count, 6e5 * count),
            name="implicit",
        )(place, owner, *matrices, mine, theirs)

    def grid_rows(start, count, rels, other, blocks):
        height = count * 36 + 8
        return pl.pallas_call(
            lambda *refs: grid_rows_kernel(start, count, rels, *refs),
            out_shape=jax.ShapeDtypeStruct((192 * count, N2), F32),
            grid_spec=pltpu.PrefetchScalarGridSpec(
                num_scalar_prefetch=2,
                grid=(len(rels), count // 2),
                in_specs=table_specs(start, count, rels) + [kept(*b.shape) for b in blocks],
                out_specs=kept(192 * count, N2),
                scratch_shapes=[pltpu.VMEM((height, NM), F32), pltpu.VMEM((160, N2), F32)],
            ),
            compiler_params=parameters(),
            cost_estimate=cost(7e7 * count * len(rels), 5e5 * count * len(rels)),
            name="grid_rows",
        )(place, owner, legendre, other, *blocks)

    def after(value, *earlier):
        return lax.optimization_barrier((value,) + earlier)[0]

    def exchange(value):
        return lax.all_to_all(value, ("core", "wave"), 0, 0, tiled=True)

    steps = [{} for _ in CHUNKS]

    def finish(now, *earlier):
        up, down = now["moving"]
        if earlier:
            up = after(up, *earlier)
        now["sum"] = now["mine"] + up + down
        now["theirs"] = lax.ppermute(now["sum"], "yh", SWAP)

    for k, (start, count) in enumerate(CHUNKS):
        now, before = steps[k], steps[k - 1] if k else None
        now["cut"] = cut = halves(count)
        away, source = aways[k], fours[k]
        if k:
            away = after(away, before["four"])
            source = after(source, before["right"], before["left"])
        now["other"] = lax.ppermute(away, "core", SWAP)
        now["four"] = four = exchange(source).reshape(192 * count, N2)
        top, bottom = spectra(start, count, (2,), four, now["other"])
        right, left, now["mine"] = spectra(start, count, (1, 3, 0), four, now["other"])
        if k:
            finish(before, now["mine"])
            top, bottom, _ = lax.optimization_barrier((top, bottom, before["sum"]))
        top = lax.ppermute(top, "z", UP)
        bottom = lax.ppermute(bottom, "z", DOWN)
        now["right"] = right = right.at[:cut].add(top)
        now["left"] = left = left.at[cut:].add(bottom)
        now["moving"] = lax.ppermute(right, "z", UP), lax.ppermute(left, "z", DOWN)
    finish(steps[-1])
    for k, (start, count) in enumerate(CHUNKS):
        now, before = steps[k], steps[k - 1] if k else None
        theirs = after(now["theirs"], *before["ends"]) if k else now["theirs"]
        now["new"] = new = implicit(start, count, now["sum"], theirs)
        if k:
            new = after(new, before["top"], before["bottom"])
        left = lax.ppermute(new, "z", UP)
        right = lax.ppermute(new, "z", DOWN)
        now["left"], now["right"] = left, right
        now["ends"] = left[: now["cut"]], right[now["cut"] :]
        now["top"] = lax.ppermute(now["ends"][0], "z", UP)
        now["bottom"] = lax.ppermute(now["ends"][1], "z", DOWN)
    results = []
    for k, (start, count) in enumerate(CHUNKS):
        now = steps[k]
        later = steps[k + 1] if k + 1 < len(CHUNKS) else None
        right, top = now["right"], now["top"]
        if later:
            right = after(right, later["new"])
        rows = grid_rows(start, count, (0, 1, 3), now["other"], (now["new"], right, now["left"]))
        rows = grid_rows(start, count, (2,), now["other"], (top, now["bottom"], rows))
        results.append(exchange(rows.reshape(16, 3, 4 * count, N2)))
    out = pl.pallas_call(
        inverse_kernel,
        out_shape=jax.ShapeDtypeStruct((3, ROWS, 6, NLON), F32),
        in_specs=[whole()] + [smem] * 2 + [whole()] * (3 + len(CHUNKS)),
        out_specs=whole(),
        scratch_shapes=[pltpu.VMEM((N1, 120, 256), F32), pltpu.VMEM((184, NM), F32)],
        compiler_params=parameters(),
        cost_estimate=cost(4e9, 8e6),
        name="inverse",
    )(owner_column, lat_weights, place, twiddle, *backward, *results)
    return out.transpose(0, 2, 1, 3)


def solution(mesh):
    fine = Mesh(mesh.devices.reshape(2, 4, 2, 8), ("yh", "z", "core", "wave"))
    lat = ("yh", "z", "core")
    rows = P(None, None, lat + ("wave",), None)
    in_specs = (rows, P(), P("wave", lat, None), P(lat), P(), P(), P(), P(), P())
    return jax.shard_map(
        per_device, mesh=fine, in_specs=in_specs, out_specs=rows, check_vma=False
    )
```

```python
import math

import jax
import jax.numpy as jnp
import numpy as np
from jax import lax
from jax.experimental import pallas as pl
from jax.experimental.pallas import tpu as pltpu
from jax.sharding import Mesh, PartitionSpec as P

NLON = 2560
NM = 1280
PAIRS = 640
LAT = 640
PACK = 1408
FL = 18
ROWS = 5
N1 = 20
N2 = 128
HALF = 40
BF = jnp.bfloat16
F32 = jnp.float32
CHUNKS = ((0, 6), (6, 4))
UP = [(i, (i + 1) % 4) for i in range(4)]
DOWN = [(i, (i + 3) % 4) for i in range(4)]
SWAP = [(0, 1), (1, 0)]
VMEM_BYTES = 40 * 1024 * 1024


def split(x):
    high = x.astype(BF)
    return high, (x - high.astype(F32)).astype(BF)


def dot3(x, weight_high, weight_low, dims):
    high, low = split(x)
    out = lax.dot_general(high, weight_high, dims, preferred_element_type=F32)
    out += lax.dot_general(low, weight_high, dims, preferred_element_type=F32)
    return out + lax.dot_general(high, weight_low, dims, preferred_element_type=F32)


NN = (((1,), (0,)), ((), ()))
NT = (((1,), (1,)), ((), ()))


def constant_tables():
    scale = math.sqrt(2.0 / NLON)
    wave1 = np.arange(N1)[:, None]
    lon2 = np.arange(N2)[None, :]
    turn = 2.0 * np.pi * ((wave1 * lon2) % NLON) / NLON
    twiddle = np.stack([np.cos(turn), np.sin(turn)]).astype(np.float32)
    angle = 2.0 * np.pi * ((np.arange(N2)[:, None] * np.arange(64)[None, :]) % N2) / N2
    cos, sin = np.cos(angle) * scale, np.sin(angle) * scale
    zero = np.zeros_like(cos)
    forward = np.concatenate(
        [
            np.concatenate([cos, zero, -sin, zero], 1),
            np.concatenate([sin, zero, cos, zero], 1),
            np.concatenate([zero, cos, zero, -sin], 1),
            np.concatenate([zero, sin, zero, cos], 1),
        ],
        0,
    ).astype(np.float32)
    backward = np.concatenate(
        [
            np.concatenate([cos.T, sin.T, zero.T, zero.T], 1),
            np.concatenate([zero.T, zero.T, cos.T, sin.T], 1),
            np.concatenate([-sin.T, cos.T, zero.T, zero.T], 1),
            np.concatenate([zero.T, zero.T, -sin.T, cos.T], 1),
        ],
        0,
    ).astype(np.float32)

    def parts(table):
        high = table.astype(jnp.bfloat16)
        return np.concatenate([high, (table - high.astype(np.float32)).astype(jnp.bfloat16)])

    return twiddle, parts(forward), parts(backward)


def lane_waves():
    lane = lax.broadcasted_iota(jnp.int32, (1, NM), 1)
    return 2 * (lane // N2) + (lane % N2) // 64 + N1 * (lane % 64)


def one_hot(owner_ref, core, start, rows):
    first = core * HALF + 4 * start
    column = [owner_ref[w * 80 + first : w * 80 + first + rows, :] for w in range(8)]
    column = jnp.concatenate(column, axis=0)[:, 0:1]
    waves = lane_waves()
    second = jnp.where(NM - 1 - column == waves, 1.0, 0.0).astype(BF)
    first = jnp.where(column == waves, 1.0, 0.0).astype(BF)
    return second, first


def fourier_kernel(place_ref, owner_ref, *refs):
    parts = len(CHUNKS)
    sources, table_ref, refs = refs[:3], refs[3], refs[4:]
    send_refs, away_refs = refs[:parts], refs[parts : 2 * parts]
    stage_ref, wide_ref, half_ref, sem = refs[2 * parts : 2 * parts + 4]
    locals_ = refs[2 * parts + 4 :]
    grid_ref, twiddle_ref, weight_ref = locals_
    loads = []
    for k in range(3):
        loads.append(pltpu.make_async_copy(sources[k], locals_[k], sem.at[2 * parts + k]))
        loads[-1].start()
    source = (1 - place_ref[0]) * HALF
    fetches, copies = [], []
    for k, (start, count) in enumerate(CHUNKS):
        rows = pl.ds(4 * start, 4 * count)
        here = table_ref.at[pl.ds(source + 4 * start, 4 * count)]
        fetches.append(pltpu.make_async_copy(here, half_ref.at[rows], sem.at[k]))
        fetches[-1].start()
        copies.append(pltpu.make_async_copy(half_ref.at[rows], away_refs[k], sem.at[parts + k]))
    loads[0].wait()
    loads[1].wait()
    for r in range(ROWS):
        tiles = [grid_ref[:, r, :, N2 * x1 : N2 * (x1 + 1)] for x1 in range(N1)]
        sums = [tiles[x1] + tiles[x1 + 10] for x1 in range(10)]
        differences = [tiles[x1] - tiles[x1 + 10] for x1 in range(10)]
        for m1 in range(11):
            source = sums if m1 % 2 == 0 else differences
            real, imag = source[0], None
            for x1 in range(1, 10):
                turn = 2.0 * math.pi * ((m1 * x1) % N1) / N1
                cos, sin = math.cos(turn), math.sin(turn)
                real = real + source[x1] * cos
                if m1 % 10:
                    term = source[x1] * (-sin)
                    imag = term if imag is None else imag + term
            if imag is None:
                imag = jnp.zeros_like(real)
            for wave, sign in ((m1, 1.0), (N1 - m1, -1.0)):
                if wave in (m1, N1) and sign < 0:
                    continue
                cos = twiddle_ref[0, wave : wave + 1, :]
                sin = twiddle_ref[1, wave : wave + 1, :]
                rotated_real = real * cos + (sign * imag) * sin
                rotated_imag = (sign * imag) * cos - real * sin
                base = (wave % 2) * 256
                rows = slice(3 * r, 3 * r + 3)
                stage_ref[wave // 2, rows, 0:6, base : base + N2] = rotated_real
                stage_ref[wave // 2, rows, 0:6, base + N2 : base + 256] = rotated_imag
    loads[2].wait()
    for fetch, copy in zip(fetches, copies):
        fetch.wait()
        copy.start()
    wide_ref[...] = jnp.zeros_like(wide_ref)
    for t in range(N1 // 2):
        out = dot3(stage_ref[t].reshape(120, 512), weight_ref[:512], weight_ref[512:], NN)
        for r in range(ROWS):
            rows = [out[r * 24 + f * 8 : r * 24 + f * 8 + 6] for f in range(3)]
            both = [row[:, :N2] for row in rows] + [row[:, N2:] for row in rows]
            both = jnp.concatenate(both, axis=0)
            wide_ref[r * 36 : r * 36 + 36, t * N2 : (t + 1) * N2] = both
    high, low = split(wide_ref[...])

    for k, (start, count) in enumerate(CHUNKS):
        group = 4 * count
        for c in range(2):
            half = 8 * group
            picks = jnp.concatenate(one_hot(owner_ref, c, start, group), axis=0)
            out = lax.dot_general(picks, high, NT, preferred_element_type=F32)
            out += lax.dot_general(picks, low, NT, preferred_element_type=F32)
            tile = [out[:half, :180], out[half:, :180], jnp.zeros((half, 24), F32)]
            tile = jnp.concatenate(tile, axis=1)
            for w in range(8):
                for t in range(3):
                    rows = slice(w * group, (w + 1) * group)
                    send_refs[k][c * 8 + w, t] = tile[rows, t * N2 : (t + 1) * N2]
    for copy in copies:
        copy.wait()


def scatter(owner_ref, got_ref, start, count):
    group = 4 * count
    total = jnp.zeros((184, NM), F32)
    for c in range(2):
        second, first = one_hot(owner_ref, c, start, group)
        tiles = [
            jnp.concatenate([got_ref[c * 8 + w, t] for w in range(8)], axis=0) for t in range(3)
        ]
        flipped = jnp.concatenate(tiles, axis=1).T
        for rows, picks in ((flipped[0:184], second), (flipped[180:364], first)):
            high, low = split(rows)
            total += lax.dot_general(high, picks, NN, preferred_element_type=F32)
            total += lax.dot_general(low, picks, NN, preferred_element_type=F32)
    return total


def scatter_kernel(owner_ref, *refs):
    total = jnp.zeros((184, NM), F32)
    for k, (start, count) in enumerate(CHUNKS[:-1]):
        total += scatter(owner_ref, refs[k], start, count)
    refs[-1][...] = total


def inverse_kernel(owner_ref, weight_ref, place_ref, twiddle_ref, table_ref, early_ref, got_ref, out_ref, stage_ref, wide_ref):
    wave = place_ref[1]
    start, count = CHUNKS[-1]
    wide_ref[...] = early_ref[...] + scatter(owner_ref, got_ref, start, count)
    for t in range(N1 // 2):
        rows = []
        for r in range(ROWS):
            block = wide_ref[r * 36 : (r + 1) * 36, t * N2 : (t + 1) * N2]
            block = block * weight_ref[wave * ROWS + r]
            gap = jnp.zeros((2, N2), F32)
            real, imag = [], []
            for f in range(3):
                real += [block[f * 6 : f * 6 + 6], gap]
                imag += [block[FL + f * 6 : FL + f * 6 + 6], gap]
            both = [jnp.concatenate(real, axis=0), jnp.concatenate(imag, axis=0)]
            rows.append(jnp.concatenate(both, axis=1))
        out = dot3(jnp.concatenate(rows, axis=0), table_ref[:256], table_ref[256:], NN)
        for odd in range(2):
            m1 = 2 * t + odd
            real = out[:, odd * 256 : odd * 256 + N2]
            imag = out[:, odd * 256 + N2 : odd * 256 + 256]
            cos = twiddle_ref[0, m1 : m1 + 1, :]
            sin = twiddle_ref[1, m1 : m1 + 1, :]
            stage_ref[m1, :, :N2] = real * cos - imag * sin
            stage_ref[m1, :, N2:] = real * sin + imag * cos
    for r in range(ROWS):
        rows = slice(r * 24, (r + 1) * 24)
        zero, ten = stage_ref[0, rows, :N2], stage_ref[10, rows, :N2]
        sums, gaps = [None], [None]
        for m in range(1, 10):
            sums.append(stage_ref[m, rows, :N2] + stage_ref[N1 - m, rows, :N2])
            gaps.append(stage_ref[m, rows, N2:] - stage_ref[N1 - m, rows, N2:])
        for x1 in range(10):
            even = zero + ten if x1 % 2 == 0 else zero - ten
            odd = jnp.zeros_like(zero)
            for m in range(1, 10):
                turn = 2.0 * math.pi * ((m * x1) % N1) / N1
                term = sums[m] * math.cos(turn) - gaps[m] * math.sin(turn)
                if m % 2 == 0:
                    even = even + term
                else:
                    odd = odd + term
            for f in range(3):
                rows6 = slice(f * 8, f * 8 + 6)
                out_ref[f, r, :, x1 * N2 : (x1 + 1) * N2] = (even + odd)[rows6]
                out_ref[f, r, :, (x1 + 10) * N2 : (x1 + 11) * N2] = (even - odd)[rows6]


def relative(rels, step):
    value = jnp.int32(rels[-1])
    for k, rel in enumerate(rels[:-1]):
        value = jnp.where(step == k, rel, value)
    return value


def spectra_kernel(start, count, rels, place_ref, owner_ref, own_ref, other_ref, four_ref, *refs):
    target, step = pl.program_id(0), pl.program_id(1)
    core, wave = place_ref[0], place_ref[1]
    z = lax.rem(place_ref[2] + relative(rels, target), 4)
    out_refs, work_ref, four_work = refs[:-2], refs[-2], refs[-1]
    extra = count * 36
    group = 4 * count

    @pl.when(step == 0)
    def _():
        work_ref[extra : extra + 8, :] = jnp.zeros((8, NM), F32)

    lane = lax.broadcasted_iota(jnp.int32, (1, NM), 1)
    narrow = lax.broadcasted_iota(jnp.int32, (1, N2), 1)
    kept = []
    for i in range(2):
        first_wave = owner_ref[wave * 80 + core * HALF + 4 * start + z * count + 2 * step + i]
        pair = z * count + 2 * step + i
        for b, band in enumerate((core, 1 - core)):
            base = band * (24 * group) + pair
            tiles = [
                four_ref[pl.ds(base + t * group, 8, stride=3 * group), :] for t in range(3)
            ]
            line = jnp.concatenate(tiles, axis=1)
            for r in range(ROWS):
                pieces = [line[:, r * 36 : r * 36 + 36], jnp.zeros((8, 4), F32)]
                pieces += [line[:, 180 + r * 36 : 216 + r * 36], jnp.zeros((8, 52), F32)]
                piece = jnp.concatenate(pieces, axis=1)
                four_work[pl.ds(i * 80 + b * HALF + r, 8, stride=ROWS), :] = piece
        four = four_work[i * 80 : (i + 1) * 80, :]
        four_high = four.astype(BF).astype(F32)
        left = jnp.concatenate([four_high, four_high, four - four_high], axis=0).T
        table = jnp.concatenate([own_ref[i], other_ref[i]], axis=0)
        main = table[:, :NM]
        main_high = main.astype(BF).astype(F32)
        right = jnp.concatenate([main_high, main - main_high, main_high], axis=0)
        both = lax.dot_general(left[:80].astype(BF), right.astype(BF), NN, preferred_element_type=F32)
        kept.append(jnp.where(lane < NM - first_wave, both[40:80], both[0:40])[:36])
        last = jnp.sum(table[:, NM : NM + 1] * four, axis=0, keepdims=True)
        spot = pl.multiple_of((2 * step + i) * N2, N2)
        work_ref[extra : extra + 1, pl.ds(spot, N2)] = jnp.where(narrow < 36, last, 0.0)
    work_ref[pl.ds(pl.multiple_of(step * 72, 8), 72), :] = jnp.concatenate(kept, axis=0)

    @pl.when(step == count // 2 - 1)
    def _():
        if len(rels) == 1:
            cut = halves(count)
            out_refs[0][...] = work_ref[:cut]
            out_refs[1][...] = work_ref[cut:]
        else:
            for k, out_ref in enumerate(out_refs):

                @pl.when(target == k)
                def _(out_ref=out_ref):
                    out_ref[...] = work_ref[...]


def halves(count):
    return (count * 36 + 8) // 16 * 8


def implicit_rows(load, degree, modes_e, modes_f, rates, height, heating):
    q = degree * (degree + 1.0) / float(NM * (NM + 1))
    rotation = 1.0 / (1.0 + 4.0 * q * q)
    damping = [1.0 / (1.0 + 4.0 * q * rates[i]) for i in range(6)]
    out = []
    for part in range(2):
        base = part * FL
        d = [load(base + 6 + l) for l in range(6)]
        t = [load(base + 12 + l) for l in range(6)]
        forced = []
        for l in range(6):
            total = d[l]
            for h in range(6):
                total = total - heating[h * 6 + l] * t[h]
            forced.append(total)
        modal = []
        for i in range(6):
            total = modes_e[i] * forced[0]
            for h in range(1, 6):
                total = total + modes_e[h * 6 + i] * forced[h]
            modal.append(total * damping[i])
        spread = []
        for l in range(6):
            total = modes_f[l] * modal[0]
            for i in range(1, 6):
                total = total + modes_f[i * 6 + l] * modal[i]
            spread.append(total)
        out += [load(base + l) * rotation for l in range(6)]
        out += spread
        for l in range(6):
            total = height[l] * spread[0]
            for h in range(1, 6):
                total = total + height[h * 6 + l] * spread[h]
            out.append(t[l] - q * total)
    return out


def implicit_kernel(start, count, place_ref, owner_ref, e_ref, f_ref, rate_ref, height_ref, heat_ref, x_ref, y_ref, out_ref):
    core, wave, z = place_ref[0], place_ref[1], place_ref[2]
    matrices = [[ref[i] for i in range(36)] for ref in (e_ref, f_ref)]
    rates = [rate_ref[i] for i in range(6)]
    heights = [[ref[i] for i in range(36)] for ref in (height_ref, heat_ref)]
    arguments = (matrices[0], matrices[1], rates, heights[0], heights[1])
    row = lax.broadcasted_iota(jnp.int32, (count, 1), 0)
    first_wave = jnp.zeros((count, 1), jnp.int32)
    for i in range(count):
        value = owner_ref[wave * 80 + core * HALF + 4 * start + z * count + i]
        first_wave = jnp.where(row == i, value, first_wave)

    tile = pl.program_id(0)
    packed = tile * N2 + lax.broadcasted_iota(jnp.int32, (count, N2), 1)
    degree = jnp.where(packed < NM - first_wave, first_wave + packed, packed - 1).astype(F32)

    def load(j):
        spot = pl.ds(j, count, stride=36)
        return x_ref[spot, :] + y_ref[spot, :]

    for j, value in enumerate(implicit_rows(load, degree, *arguments)):
        out_ref[pl.ds(j, count, stride=36), :] = value
    extra = count * 36
    line = x_ref[extra : extra + 1, :] + y_ref[extra : extra + 1, :]
    flipped = jnp.broadcast_to(line, (8, N2)).T
    degree = jnp.full((1, 8), NM - 1.0, F32)
    values = implicit_rows(lambda j: flipped[j : j + 1], degree, *arguments)
    values.append(jnp.zeros((N2 - 36, 8), F32))
    out_ref[extra : extra + 8, :] = jnp.concatenate(values, axis=0).T


def grid_rows_kernel(start, count, rels, place_ref, owner_ref, own_ref, other_ref, *refs):
    target, step = pl.program_id(0), pl.program_id(1)
    core, wave = place_ref[0], place_ref[1]
    z = lax.rem(place_ref[2] + relative(rels, target), 4)
    out_ref, work_ref, back_work = refs[-3:]
    if len(rels) == 1:
        top_ref, bottom_ref, before_ref = refs[:-3]
    else:
        spec_refs = refs[:-3]
    extra = count * 36
    group = 4 * count
    cut = halves(count)

    for k in range(len(rels)):

        @pl.when((target == k) & (step == 0))
        def _(k=k):
            if len(rels) == 1:
                work_ref[:cut] = top_ref[...]
                work_ref[cut:] = bottom_ref[...]
                out_ref[...] = before_ref[...]
            else:
                work_ref[...] = spec_refs[k][...]

    lane = lax.broadcasted_iota(jnp.int32, (1, NM), 1)
    block = work_ref[pl.ds(pl.multiple_of(step * 72, 8), 72), :]
    pad = jnp.zeros((4, NM), F32)
    for i in range(2):
        first_wave = owner_ref[wave * 80 + core * HALF + 4 * start + z * count + 2 * step + i]
        pair = z * count + 2 * step + i
        values = jnp.concatenate([block[i * 36 : i * 36 + 36], pad], axis=0)
        is_first = lane < NM - first_wave
        both = jnp.concatenate(
            [jnp.where(is_first, 0.0, values), jnp.where(is_first, values, 0.0)], axis=0
        )
        high, low = split(both)
        table = jnp.concatenate([own_ref[i], other_ref[i]], axis=0)
        back = dot3(table[:, :NM], high, low, NT)
        back = jnp.concatenate([back, jnp.zeros((80, 48), F32)], axis=1)
        spot = pl.multiple_of((2 * step + i) * N2, N2)
        last = work_ref[extra : extra + 1, pl.ds(spot, N2)]
        back = back + table[:, NM : NM + 1] * last
        back_work[i * 80 : (i + 1) * 80, :] = back
        for b, band in enumerate((core, 1 - core)):
            rows = [
                back_work[pl.ds(i * 80 + b * HALF + r, 8, stride=ROWS), :] for r in range(ROWS)
            ]
            line = [row[:, 0:36] for row in rows] + [row[:, 40:76] for row in rows]
            line = jnp.concatenate(line + [jnp.zeros((8, 24), F32)], axis=1)
            base = band * (24 * group) + pair
            for t in range(3):
                spot = pl.ds(base + t * group, 8, stride=3 * group)
                out_ref[spot, :] = line[:, t * N2 : (t + 1) * N2]


def fold_kernel(right_ref, top_ref, left_ref, bottom_ref, right_out, left_out):
    cut = top_ref.shape[0]
    right_out[:cut] = right_ref[:cut] + top_ref[...]
    right_out[cut:] = right_ref[cut:]
    left_out[:cut] = left_ref[:cut]
    left_out[cut:] = left_ref[cut:] + bottom_ref[...]


def sum_kernel(x_ref, y_ref, z_ref, out_ref):
    out_ref[...] = x_ref[...] + y_ref[...] + z_ref[...]


def parameters():
    return pltpu.CompilerParams(vmem_limit_bytes=VMEM_BYTES)


def whole(space=pltpu.VMEM):
    return pl.BlockSpec(memory_space=space)


def cost(flops, size):
    return pl.CostEstimate(flops=int(flops), bytes_accessed=int(size), transcendentals=0)


def per_device(
    grad_grid, owner, legendre, lat_weights, modes_e, modes_f, rates, height_matrix, heating_matrix
):
    core, wave, z = lax.axis_index("core"), lax.axis_index("wave"), lax.axis_index("z")
    twiddle, forward, backward = constant_tables()
    smem = whole(pltpu.SMEM)
    place = jnp.stack([core, wave, z]).astype(jnp.int32)
    owner_column = jnp.broadcast_to(owner[:, None], (PAIRS, N2))
    matrices = [m.reshape(36) for m in (modes_e, modes_f)] + [rates]
    matrices += [m.reshape(36) for m in (height_matrix, heating_matrix)]

    made = pl.pallas_call(
        fourier_kernel,
        out_shape=[jax.ShapeDtypeStruct((16, 3, 4 * n, N2), F32) for _, n in CHUNKS]
        + [jax.ShapeDtypeStruct((4 * n, HALF, PACK), F32) for _, n in CHUNKS],
        in_specs=[smem, whole()] + [whole(pltpu.HBM)] * 4,
        out_specs=[whole()] * len(CHUNKS) + [whole(pltpu.HBM)] * len(CHUNKS),
        scratch_shapes=[
            pltpu.VMEM((10, 15, 8, 512), F32),
            pltpu.VMEM((184, NM), F32),
            pltpu.VMEM((HALF, HALF, PACK), F32),
            pltpu.SemaphoreType.DMA((2 * len(CHUNKS) + 3,)),
            pltpu.VMEM((3, ROWS, 6, NLON), F32),
            pltpu.VMEM((2, N1, N2), F32),
            pltpu.VMEM((1024, 256), BF),
        ],
        compiler_params=parameters(),
        cost_estimate=cost(4e9, 2.6e7),
        name="fourier",
    )(place, owner_column, grad_grid.transpose(0, 2, 1, 3), twiddle, forward, legendre)
    fours, aways = made[: len(CHUNKS)], made[len(CHUNKS) :]

    def zone(rels, t, place):
        return lax.rem(place[2] + relative(rels, t), 4)

    def table_specs(start, count, rels):
        return [
            pl.BlockSpec(
                (2, HALF, PACK),
                lambda t, s, place, owner: (
                    place[0] * 20 + 2 * start + zone(rels, t, place) * (count // 2) + s,
                    0,
                    0,
                ),
            ),
            pl.BlockSpec(
                (2, HALF, PACK),
                lambda t, s, place, owner: (zone(rels, t, place) * (count // 2) + s, 0, 0),
            ),
        ]

    def kept(rows, lanes):
        return pl.BlockSpec((rows, lanes), lambda t, s, place, owner: (0, 0))

    def spectra(start, count, rels, four, other):
        height = count * 36 + 8
        cut = halves(count)
        rows = [cut, height - cut] if len(rels) == 1 else [height] * len(rels)
        return pl.pallas_call(
            lambda *refs: spectra_kernel(start, count, rels, *refs),
            out_shape=[jax.ShapeDtypeStruct((n, NM), F32) for n in rows],
            grid_spec=pltpu.PrefetchScalarGridSpec(
                num_scalar_prefetch=2,
                grid=(len(rels), count // 2),
                in_specs=table_specs(start, count, rels) + [kept(192 * count, N2)],
                out_specs=[kept(n, NM) for n in rows],
                scratch_shapes=[pltpu.VMEM((height, NM), F32), pltpu.VMEM((160, N2), F32)],
            ),
            compiler_params=parameters(),
            cost_estimate=cost(5e7 * count * len(rels), 5e5 * count * len(rels)),
            name="spectra",
        )(place, owner, legendre, other, four)

    def implicit(start, count, mine, theirs):
        height = count * 36 + 8
        return pl.pallas_call(
            lambda *refs: implicit_kernel(start, count, *refs),
            out_shape=jax.ShapeDtypeStruct((height, NM), F32),
            grid=(10,),
            in_specs=[smem] * 7 + [pl.BlockSpec((height, N2), lambda t: (0, t))] * 2,
            out_specs=pl.BlockSpec((height, N2), lambda t: (0, t)),
            compiler_params=parameters(),
            cost_estimate=cost(1e7 * count, 6e5 * count),
            name="implicit",
        )(place, owner, *matrices, mine, theirs)

    def grid_rows(start, count, rels, other, blocks):
        height = count * 36 + 8
        return pl.pallas_call(
            lambda *refs: grid_rows_kernel(start, count, rels, *refs),
            out_shape=jax.ShapeDtypeStruct((192 * count, N2), F32),
            grid_spec=pltpu.PrefetchScalarGridSpec(
                num_scalar_prefetch=2,
                grid=(len(rels), count // 2),
                in_specs=table_specs(start, count, rels) + [kept(*b.shape) for b in blocks],
                out_specs=kept(192 * count, N2),
                scratch_shapes=[pltpu.VMEM((height, NM), F32), pltpu.VMEM((160, N2), F32)],
            ),
            compiler_params=parameters(),
            cost_estimate=cost(7e7 * count * len(rels), 5e5 * count * len(rels)),
            name="grid_rows",
        )(place, owner, legendre, other, *blocks)

    def after(value, *earlier):
        return lax.optimization_barrier((value,) + earlier)[0]

    def exchange(value):
        return lax.all_to_all(value, ("core", "wave"), 0, 0, tiled=True)

    steps = [{} for _ in CHUNKS]

    def finish(now, *earlier):
        up, down = now["moving"]
        if earlier:
            up = after(up, *earlier)
        now["sum"] = now["mine"] + up + down
        now["theirs"] = lax.ppermute(now["sum"], "yh", SWAP)

    for k, (start, count) in enumerate(CHUNKS):
        now, before = steps[k], steps[k - 1] if k else None
        now["cut"] = cut = halves(count)
        away, source = aways[k], fours[k]
        if k:
            away = after(away, before["four"])
            source = after(source, before["right"], before["left"])
        now["other"] = lax.ppermute(away, "core", SWAP)
        now["four"] = four = exchange(source).reshape(192 * count, N2)
        top, bottom = spectra(start, count, (2,), four, now["other"])
        right, left, now["mine"] = spectra(start, count, (1, 3, 0), four, now["other"])
        if k:
            finish(before, now["mine"])
            top, bottom, _ = lax.optimization_barrier((top, bottom, before["sum"]))
        top = lax.ppermute(top, "z", UP)
        bottom = lax.ppermute(bottom, "z", DOWN)
        if k:
            right, left = right.at[:cut].add(top), left.at[cut:].add(bottom)
        else:
            right, left = pl.pallas_call(
                fold_kernel,
                out_shape=[jax.ShapeDtypeStruct(right.shape, F32)] * 2,
                in_specs=[whole()] * 4,
                out_specs=[whole()] * 2,
                compiler_params=parameters(),
                cost_estimate=cost(1e5, 1e6),
                name="fold",
            )(right, top, left, bottom)
        now["right"], now["left"] = right, left
        now["moving"] = lax.ppermute(right, "z", UP), lax.ppermute(left, "z", DOWN)
    finish(steps[-1])
    for k, (start, count) in enumerate(CHUNKS):
        now, before = steps[k], steps[k - 1] if k else None
        theirs = after(now["theirs"], *before["ends"]) if k else now["theirs"]
        now["new"] = new = implicit(start, count, now["sum"], theirs)
        if k:
            new = after(new, before["top"], before["bottom"])
        left = lax.ppermute(new, "z", UP)
        right = lax.ppermute(new, "z", DOWN)
        now["left"], now["right"] = left, right
        now["ends"] = left[: now["cut"]], right[now["cut"] :]
        now["top"] = lax.ppermute(now["ends"][0], "z", UP)
        now["bottom"] = lax.ppermute(now["ends"][1], "z", DOWN)
    results = []
    for k, (start, count) in enumerate(CHUNKS):
        now = steps[k]
        later = steps[k + 1] if k + 1 < len(CHUNKS) else None
        right, top = now["right"], now["top"]
        if later:
            right = after(right, later["new"])
        rows = grid_rows(start, count, (0, 1, 3), now["other"], (now["new"], right, now["left"]))
        rows = grid_rows(start, count, (2,), now["other"], (top, now["bottom"], rows))
        results.append(exchange(rows.reshape(16, 3, 4 * count, N2)))
    early = pl.pallas_call(
        scatter_kernel,
        out_shape=jax.ShapeDtypeStruct((184, NM), F32),
        in_specs=[whole()] * len(CHUNKS),
        out_specs=whole(),
        compiler_params=parameters(),
        cost_estimate=cost(1e9, 2e6),
        name="scatter",
    )(owner_column, *results[:-1])
    out = pl.pallas_call(
        inverse_kernel,
        out_shape=jax.ShapeDtypeStruct((3, ROWS, 6, NLON), F32),
        in_specs=[whole()] + [smem] * 2 + [whole()] * 4,
        out_specs=whole(),
        scratch_shapes=[pltpu.VMEM((N1, 120, 256), F32), pltpu.VMEM((184, NM), F32)],
        compiler_params=parameters(),
        cost_estimate=cost(4e9, 8e6),
        name="inverse",
    )(owner_column, lat_weights, place, twiddle, backward, early, results[-1])
    return out.transpose(0, 2, 1, 3)


def solution(mesh):
    fine = Mesh(mesh.devices.reshape(2, 4, 2, 8), ("yh", "z", "core", "wave"))
    lat = ("yh", "z", "core")
    rows = P(None, None, lat + ("wave",), None)
    in_specs = (rows, P(), P("wave", lat, None), P(lat), P(), P(), P(), P(), P())
    return jax.shard_map(
        per_device, mesh=fine, in_specs=in_specs, out_specs=rows, check_vma=False
    )
```

```python
import math

import jax
import jax.numpy as jnp
import numpy as np
from jax import lax
from jax.experimental import pallas as pl
from jax.experimental.pallas import tpu as pltpu
from jax.sharding import Mesh, PartitionSpec as P

NLON = 2560
NM = 1280
PAIRS = 640
LAT = 640
PACK = 1408
FL = 18
ROWS = 5
N1 = 20
N2 = 128
HALF = 40
BF = jnp.bfloat16
F32 = jnp.float32
CHUNKS = ((0, 6), (6, 4))
UP = [(i, (i + 1) % 4) for i in range(4)]
DOWN = [(i, (i + 3) % 4) for i in range(4)]
SWAP = [(0, 1), (1, 0)]
VMEM_BYTES = 40 * 1024 * 1024


def split(x):
    high = x.astype(BF)
    return high, (x - high.astype(F32)).astype(BF)


def dot3(x, weight_high, weight_low, dims):
    high, low = split(x)
    out = lax.dot_general(high, weight_high, dims, preferred_element_type=F32)
    out += lax.dot_general(low, weight_high, dims, preferred_element_type=F32)
    return out + lax.dot_general(high, weight_low, dims, preferred_element_type=F32)


NN = (((1,), (0,)), ((), ()))
NT = (((1,), (1,)), ((), ()))


def constant_tables():
    scale = math.sqrt(2.0 / NLON)
    wave1 = np.arange(N1)[:, None]
    lon2 = np.arange(N2)[None, :]
    turn = 2.0 * np.pi * ((wave1 * lon2) % NLON) / NLON
    twiddle = np.stack([np.cos(turn), np.sin(turn)]).astype(np.float32)
    angle = 2.0 * np.pi * ((np.arange(N2)[:, None] * np.arange(64)[None, :]) % N2) / N2
    cos, sin = np.cos(angle) * scale, np.sin(angle) * scale
    zero = np.zeros_like(cos)
    forward = np.concatenate(
        [
            np.concatenate([cos, zero, -sin, zero], 1),
            np.concatenate([sin, zero, cos, zero], 1),
            np.concatenate([zero, cos, zero, -sin], 1),
            np.concatenate([zero, sin, zero, cos], 1),
        ],
        0,
    ).astype(np.float32)
    backward = np.concatenate(
        [
            np.concatenate([cos.T, sin.T, zero.T, zero.T], 1),
            np.concatenate([zero.T, zero.T, cos.T, sin.T], 1),
            np.concatenate([-sin.T, cos.T, zero.T, zero.T], 1),
            np.concatenate([zero.T, zero.T, -sin.T, cos.T], 1),
        ],
        0,
    ).astype(np.float32)

    def parts(table):
        high = table.astype(jnp.bfloat16)
        return np.concatenate([high, (table - high.astype(np.float32)).astype(jnp.bfloat16)])

    return twiddle, parts(forward), parts(backward)


def lane_waves():
    lane = lax.broadcasted_iota(jnp.int32, (1, NM), 1)
    return 2 * (lane // N2) + (lane % N2) // 64 + N1 * (lane % 64)


def one_hot(owner_ref, core, start, rows):
    first = core * HALF + 4 * start
    column = [owner_ref[w * 80 + first : w * 80 + first + rows, :] for w in range(8)]
    column = jnp.concatenate(column, axis=0)[:, 0:1]
    waves = lane_waves()
    second = jnp.where(NM - 1 - column == waves, 1.0, 0.0).astype(BF)
    first = jnp.where(column == waves, 1.0, 0.0).astype(BF)
    return second, first


def fourier_kernel(place_ref, owner_ref, *refs):
    parts = len(CHUNKS)
    sources, table_ref, refs = refs[:3], refs[3], refs[4:]
    send_refs, away_refs = refs[:parts], refs[parts : 2 * parts]
    stage_ref, wide_ref, half_ref, sem = refs[2 * parts : 2 * parts + 4]
    locals_ = refs[2 * parts + 4 :]
    grid_ref, twiddle_ref, weight_ref = locals_
    loads = []
    for k in range(3):
        loads.append(pltpu.make_async_copy(sources[k], locals_[k], sem.at[2 * parts + k]))
        loads[-1].start()
    source = (1 - place_ref[0]) * HALF
    fetches, copies = [], []
    for k, (start, count) in enumerate(CHUNKS):
        rows = pl.ds(4 * start, 4 * count)
        here = table_ref.at[pl.ds(source + 4 * start, 4 * count)]
        fetches.append(pltpu.make_async_copy(here, half_ref.at[rows], sem.at[k]))
        fetches[-1].start()
        copies.append(pltpu.make_async_copy(half_ref.at[rows], away_refs[k], sem.at[parts + k]))
    loads[0].wait()
    loads[1].wait()
    for r in range(ROWS):
        tiles = [grid_ref[:, r, :, N2 * x1 : N2 * (x1 + 1)] for x1 in range(N1)]
        sums = [tiles[x1] + tiles[x1 + 10] for x1 in range(10)]
        differences = [tiles[x1] - tiles[x1 + 10] for x1 in range(10)]
        for m1 in range(11):
            source = sums if m1 % 2 == 0 else differences
            real, imag = source[0], None
            for x1 in range(1, 10):
                turn = 2.0 * math.pi * ((m1 * x1) % N1) / N1
                cos, sin = math.cos(turn), math.sin(turn)
                real = real + source[x1] * cos
                if m1 % 10:
                    term = source[x1] * (-sin)
                    imag = term if imag is None else imag + term
            if imag is None:
                imag = jnp.zeros_like(real)
            for wave, sign in ((m1, 1.0), (N1 - m1, -1.0)):
                if wave in (m1, N1) and sign < 0:
                    continue
                cos = twiddle_ref[0, wave : wave + 1, :]
                sin = twiddle_ref[1, wave : wave + 1, :]
                rotated_real = real * cos + (sign * imag) * sin
                rotated_imag = (sign * imag) * cos - real * sin
                base = (wave % 2) * 256
                rows = slice(3 * r, 3 * r + 3)
                stage_ref[wave // 2, rows, 0:6, base : base + N2] = rotated_real
                stage_ref[wave // 2, rows, 0:6, base + N2 : base + 256] = rotated_imag
    loads[2].wait()
    for fetch, copy in zip(fetches, copies):
        fetch.wait()
        copy.start()
    wide_ref[...] = jnp.zeros_like(wide_ref)
    for t in range(N1 // 2):
        out = dot3(stage_ref[t].reshape(120, 512), weight_ref[:512], weight_ref[512:], NN)
        for r in range(ROWS):
            rows = [out[r * 24 + f * 8 : r * 24 + f * 8 + 6] for f in range(3)]
            both = [row[:, :N2] for row in rows] + [row[:, N2:] for row in rows]
            both = jnp.concatenate(both, axis=0)
            wide_ref[r * 36 : r * 36 + 36, t * N2 : (t + 1) * N2] = both
    high, low = split(wide_ref[...])

    for k, (start, count) in enumerate(CHUNKS):
        group = 4 * count
        for c in range(2):
            half = 8 * group
            picks = jnp.concatenate(one_hot(owner_ref, c, start, group), axis=0)
            out = lax.dot_general(picks, high, NT, preferred_element_type=F32)
            out += lax.dot_general(picks, low, NT, preferred_element_type=F32)
            tile = [out[:half, :180], out[half:, :180], jnp.zeros((half, 24), F32)]
            tile = jnp.concatenate(tile, axis=1)
            for w in range(8):
                for t in range(3):
                    rows = slice(w * group, (w + 1) * group)
                    send_refs[k][c * 8 + w, t] = tile[rows, t * N2 : (t + 1) * N2]
    for copy in copies:
        copy.wait()


def scatter(owner_ref, got_ref, start, count):
    group = 4 * count
    total = jnp.zeros((184, NM), F32)
    for c in range(2):
        second, first = one_hot(owner_ref, c, start, group)
        tiles = [
            jnp.concatenate([got_ref[c * 8 + w, t] for w in range(8)], axis=0) for t in range(3)
        ]
        flipped = jnp.concatenate(tiles, axis=1).T
        for rows, picks in ((flipped[0:184], second), (flipped[180:364], first)):
            high, low = split(rows)
            total += lax.dot_general(high, picks, NN, preferred_element_type=F32)
            total += lax.dot_general(low, picks, NN, preferred_element_type=F32)
    return total


def scatter_kernel(owner_ref, *refs):
    total = jnp.zeros((184, NM), F32)
    for k, (start, count) in enumerate(CHUNKS[:-1]):
        total += scatter(owner_ref, refs[k], start, count)
    refs[-1][...] = total


def inverse_kernel(owner_ref, weight_ref, place_ref, twiddle_ref, table_ref, early_ref, got_ref, out_ref, stage_ref, wide_ref):
    wave = place_ref[1]
    start, count = CHUNKS[-1]
    wide_ref[...] = early_ref[...] + scatter(owner_ref, got_ref, start, count)
    for t in range(N1 // 2):
        rows = []
        for r in range(ROWS):
            block = wide_ref[r * 36 : (r + 1) * 36, t * N2 : (t + 1) * N2]
            block = block * weight_ref[wave * ROWS + r]
            gap = jnp.zeros((2, N2), F32)
            real, imag = [], []
            for f in range(3):
                real += [block[f * 6 : f * 6 + 6], gap]
                imag += [block[FL + f * 6 : FL + f * 6 + 6], gap]
            both = [jnp.concatenate(real, axis=0), jnp.concatenate(imag, axis=0)]
            rows.append(jnp.concatenate(both, axis=1))
        out = dot3(jnp.concatenate(rows, axis=0), table_ref[:256], table_ref[256:], NN)
        for odd in range(2):
            m1 = 2 * t + odd
            real = out[:, odd * 256 : odd * 256 + N2]
            imag = out[:, odd * 256 + N2 : odd * 256 + 256]
            cos = twiddle_ref[0, m1 : m1 + 1, :]
            sin = twiddle_ref[1, m1 : m1 + 1, :]
            stage_ref[m1, :, :N2] = real * cos - imag * sin
            stage_ref[m1, :, N2:] = real * sin + imag * cos
    for r in range(ROWS):
        rows = slice(r * 24, (r + 1) * 24)
        zero, ten = stage_ref[0, rows, :N2], stage_ref[10, rows, :N2]
        sums, gaps = [None], [None]
        for m in range(1, 10):
            sums.append(stage_ref[m, rows, :N2] + stage_ref[N1 - m, rows, :N2])
            gaps.append(stage_ref[m, rows, N2:] - stage_ref[N1 - m, rows, N2:])
        for x1 in range(10):
            even = zero + ten if x1 % 2 == 0 else zero - ten
            odd = jnp.zeros_like(zero)
            for m in range(1, 10):
                turn = 2.0 * math.pi * ((m * x1) % N1) / N1
                term = sums[m] * math.cos(turn) - gaps[m] * math.sin(turn)
                if m % 2 == 0:
                    even = even + term
                else:
                    odd = odd + term
            for f in range(3):
                rows6 = slice(f * 8, f * 8 + 6)
                out_ref[f, r, :, x1 * N2 : (x1 + 1) * N2] = (even + odd)[rows6]
                out_ref[f, r, :, (x1 + 10) * N2 : (x1 + 11) * N2] = (even - odd)[rows6]


def relative(rels, step):
    value = jnp.int32(rels[-1])
    for k, rel in enumerate(rels[:-1]):
        value = jnp.where(step == k, rel, value)
    return value


def spectra_kernel(start, count, rels, place_ref, owner_ref, own_ref, other_ref, four_ref, *refs):
    target, step = pl.program_id(0), pl.program_id(1)
    core, wave = place_ref[0], place_ref[1]
    z = lax.rem(place_ref[2] + relative(rels, target), 4)
    out_refs, work_ref, four_work = refs[:-2], refs[-2], refs[-1]
    extra = count * 36
    group = 4 * count

    @pl.when(step == 0)
    def _():
        work_ref[extra : extra + 8, :] = jnp.zeros((8, NM), F32)

    lane = lax.broadcasted_iota(jnp.int32, (1, NM), 1)
    narrow = lax.broadcasted_iota(jnp.int32, (1, N2), 1)
    kept = []
    for i in range(2):
        first_wave = owner_ref[wave * 80 + core * HALF + 4 * start + z * count + 2 * step + i]
        pair = z * count + 2 * step + i
        for b, band in enumerate((core, 1 - core)):
            base = band * (24 * group) + pair
            tiles = [
                four_ref[pl.ds(base + t * group, 8, stride=3 * group), :] for t in range(3)
            ]
            line = jnp.concatenate(tiles, axis=1)
            for r in range(ROWS):
                pieces = [line[:, r * 36 : r * 36 + 36], jnp.zeros((8, 4), F32)]
                pieces += [line[:, 180 + r * 36 : 216 + r * 36], jnp.zeros((8, 52), F32)]
                piece = jnp.concatenate(pieces, axis=1)
                four_work[pl.ds(i * 80 + b * HALF + r, 8, stride=ROWS), :] = piece
        four = four_work[i * 80 : (i + 1) * 80, :]
        four_high = four.astype(BF).astype(F32)
        left = jnp.concatenate([four_high, four_high, four - four_high], axis=0).T
        table = jnp.concatenate([own_ref[i], other_ref[i]], axis=0)
        main = table[:, :NM]
        main_high = main.astype(BF).astype(F32)
        right = jnp.concatenate([main_high, main - main_high, main_high], axis=0)
        both = lax.dot_general(left[:80].astype(BF), right.astype(BF), NN, preferred_element_type=F32)
        kept.append(jnp.where(lane < NM - first_wave, both[40:80], both[0:40])[:36])
        last = jnp.sum(table[:, NM : NM + 1] * four, axis=0, keepdims=True)
        spot = pl.multiple_of((2 * step + i) * N2, N2)
        work_ref[extra : extra + 1, pl.ds(spot, N2)] = jnp.where(narrow < 36, last, 0.0)
    work_ref[pl.ds(pl.multiple_of(step * 72, 8), 72), :] = jnp.concatenate(kept, axis=0)

    @pl.when(step == count // 2 - 1)
    def _():
        if len(rels) == 1:
            cut = halves(count)
            out_refs[0][...] = work_ref[:cut]
            out_refs[1][...] = work_ref[cut:]
        else:
            for k, out_ref in enumerate(out_refs):

                @pl.when(target == k)
                def _(out_ref=out_ref):
                    out_ref[...] = work_ref[...]


def halves(count):
    return (count * 36 + 8) // 16 * 8


def implicit_rows(load, degree, modes_e, modes_f, rates, height, heating):
    q = degree * (degree + 1.0) / float(NM * (NM + 1))
    rotation = 1.0 / (1.0 + 4.0 * q * q)
    damping = [1.0 / (1.0 + 4.0 * q * rates[i]) for i in range(6)]
    out = []
    for part in range(2):
        base = part * FL
        d = [load(base + 6 + l) for l in range(6)]
        t = [load(base + 12 + l) for l in range(6)]
        forced = []
        for l in range(6):
            total = d[l]
            for h in range(6):
                total = total - heating[h * 6 + l] * t[h]
            forced.append(total)
        modal = []
        for i in range(6):
            total = modes_e[i] * forced[0]
            for h in range(1, 6):
                total = total + modes_e[h * 6 + i] * forced[h]
            modal.append(total * damping[i])
        spread = []
        for l in range(6):
            total = modes_f[l] * modal[0]
            for i in range(1, 6):
                total = total + modes_f[i * 6 + l] * modal[i]
            spread.append(total)
        out += [load(base + l) * rotation for l in range(6)]
        out += spread
        for l in range(6):
            total = height[l] * spread[0]
            for h in range(1, 6):
                total = total + height[h * 6 + l] * spread[h]
            out.append(t[l] - q * total)
    return out


def implicit_kernel(start, count, place_ref, owner_ref, e_ref, f_ref, rate_ref, height_ref, heat_ref, x_ref, y_ref, out_ref):
    core, wave, z = place_ref[0], place_ref[1], place_ref[2]
    matrices = [[ref[i] for i in range(36)] for ref in (e_ref, f_ref)]
    rates = [rate_ref[i] for i in range(6)]
    heights = [[ref[i] for i in range(36)] for ref in (height_ref, heat_ref)]
    arguments = (matrices[0], matrices[1], rates, heights[0], heights[1])
    row = lax.broadcasted_iota(jnp.int32, (count, 1), 0)
    first_wave = jnp.zeros((count, 1), jnp.int32)
    for i in range(count):
        value = owner_ref[wave * 80 + core * HALF + 4 * start + z * count + i]
        first_wave = jnp.where(row == i, value, first_wave)

    tile = pl.program_id(0)
    packed = tile * N2 + lax.broadcasted_iota(jnp.int32, (count, N2), 1)
    degree = jnp.where(packed < NM - first_wave, first_wave + packed, packed - 1).astype(F32)

    def load(j):
        spot = pl.ds(j, count, stride=36)
        return x_ref[spot, :] + y_ref[spot, :]

    for j, value in enumerate(implicit_rows(load, degree, *arguments)):
        out_ref[pl.ds(j, count, stride=36), :] = value
    extra = count * 36
    line = x_ref[extra : extra + 1, :] + y_ref[extra : extra + 1, :]
    flipped = jnp.broadcast_to(line, (8, N2)).T
    degree = jnp.full((1, 8), NM - 1.0, F32)
    values = implicit_rows(lambda j: flipped[j : j + 1], degree, *arguments)
    values.append(jnp.zeros((N2 - 36, 8), F32))
    out_ref[extra : extra + 8, :] = jnp.concatenate(values, axis=0).T


def grid_rows_kernel(start, count, rels, place_ref, owner_ref, own_ref, other_ref, *refs):
    target, step = pl.program_id(0), pl.program_id(1)
    core, wave = place_ref[0], place_ref[1]
    z = lax.rem(place_ref[2] + relative(rels, target), 4)
    out_ref, work_ref, back_work = refs[-3:]
    if len(rels) == 1:
        top_ref, bottom_ref, before_ref = refs[:-3]
    else:
        spec_refs = refs[:-3]
    extra = count * 36
    group = 4 * count
    cut = halves(count)

    for k in range(len(rels)):

        @pl.when((target == k) & (step == 0))
        def _(k=k):
            if len(rels) == 1:
                work_ref[:cut] = top_ref[...]
                work_ref[cut:] = bottom_ref[...]
                out_ref[...] = before_ref[...]
            else:
                work_ref[...] = spec_refs[k][...]

    lane = lax.broadcasted_iota(jnp.int32, (1, NM), 1)
    block = work_ref[pl.ds(pl.multiple_of(step * 72, 8), 72), :]
    pad = jnp.zeros((4, NM), F32)
    for i in range(2):
        first_wave = owner_ref[wave * 80 + core * HALF + 4 * start + z * count + 2 * step + i]
        pair = z * count + 2 * step + i
        values = jnp.concatenate([block[i * 36 : i * 36 + 36], pad], axis=0)
        is_first = lane < NM - first_wave
        both = jnp.concatenate(
            [jnp.where(is_first, 0.0, values), jnp.where(is_first, values, 0.0)], axis=0
        )
        high, low = split(both)
        table = jnp.concatenate([own_ref[i], other_ref[i]], axis=0)
        back = dot3(table[:, :NM], high, low, NT)
        back = jnp.concatenate([back, jnp.zeros((80, 48), F32)], axis=1)
        spot = pl.multiple_of((2 * step + i) * N2, N2)
        last = work_ref[extra : extra + 1, pl.ds(spot, N2)]
        back = back + table[:, NM : NM + 1] * last
        back_work[i * 80 : (i + 1) * 80, :] = back
        for b, band in enumerate((core, 1 - core)):
            rows = [
                back_work[pl.ds(i * 80 + b * HALF + r, 8, stride=ROWS), :] for r in range(ROWS)
            ]
            line = [row[:, 0:36] for row in rows] + [row[:, 40:76] for row in rows]
            line = jnp.concatenate(line + [jnp.zeros((8, 24), F32)], axis=1)
            base = band * (24 * group) + pair
            for t in range(3):
                spot = pl.ds(base + t * group, 8, stride=3 * group)
                out_ref[spot, :] = line[:, t * N2 : (t + 1) * N2]


def fold_kernel(right_ref, top_ref, left_ref, bottom_ref, right_out, left_out):
    cut = top_ref.shape[0]
    right_out[:cut] = right_ref[:cut] + top_ref[...]
    right_out[cut:] = right_ref[cut:]
    left_out[:cut] = left_ref[:cut]
    left_out[cut:] = left_ref[cut:] + bottom_ref[...]


def sum_kernel(x_ref, y_ref, z_ref, out_ref):
    out_ref[...] = x_ref[...] + y_ref[...] + z_ref[...]


def parameters():
    return pltpu.CompilerParams(vmem_limit_bytes=VMEM_BYTES)


def whole(space=pltpu.VMEM):
    return pl.BlockSpec(memory_space=space)


def cost(flops, size):
    return pl.CostEstimate(flops=int(flops), bytes_accessed=int(size), transcendentals=0)


def per_device(
    grad_grid, owner, legendre, lat_weights, modes_e, modes_f, rates, height_matrix, heating_matrix
):
    core, wave, z = lax.axis_index("core"), lax.axis_index("wave"), lax.axis_index("z")
    twiddle, forward, backward = constant_tables()
    smem = whole(pltpu.SMEM)
    place = jnp.stack([core, wave, z]).astype(jnp.int32)
    owner_column = jnp.broadcast_to(owner[:, None], (PAIRS, N2))
    matrices = [m.reshape(36) for m in (modes_e, modes_f)] + [rates]
    matrices += [m.reshape(36) for m in (height_matrix, heating_matrix)]

    made = pl.pallas_call(
        fourier_kernel,
        out_shape=[jax.ShapeDtypeStruct((16, 3, 4 * n, N2), F32) for _, n in CHUNKS]
        + [jax.ShapeDtypeStruct((4 * n, HALF, PACK), F32) for _, n in CHUNKS],
        in_specs=[smem, whole()] + [whole(pltpu.HBM)] * 4,
        out_specs=[whole()] * len(CHUNKS) + [whole(pltpu.HBM)] * len(CHUNKS),
        scratch_shapes=[
            pltpu.VMEM((10, 15, 8, 512), F32),
            pltpu.VMEM((184, NM), F32),
            pltpu.VMEM((HALF, HALF, PACK), F32),
            pltpu.SemaphoreType.DMA((2 * len(CHUNKS) + 3,)),
            pltpu.VMEM((3, ROWS, 6, NLON), F32),
            pltpu.VMEM((2, N1, N2), F32),
            pltpu.VMEM((1024, 256), BF),
        ],
        compiler_params=parameters(),
        cost_estimate=cost(4e9, 2.6e7),
        name="fourier",
    )(place, owner_column, grad_grid.transpose(0, 2, 1, 3), twiddle, forward, legendre)
    fours, aways = made[: len(CHUNKS)], made[len(CHUNKS) :]

    def zone(rels, t, place):
        return lax.rem(place[2] + relative(rels, t), 4)

    def table_specs(start, count, rels):
        return [
            pl.BlockSpec(
                (2, HALF, PACK),
                lambda t, s, place, owner: (
                    place[0] * 20 + 2 * start + zone(rels, t, place) * (count // 2) + s,
                    0,
                    0,
                ),
            ),
            pl.BlockSpec(
                (2, HALF, PACK),
                lambda t, s, place, owner: (zone(rels, t, place) * (count // 2) + s, 0, 0),
            ),
        ]

    def kept(rows, lanes):
        return pl.BlockSpec((rows, lanes), lambda t, s, place, owner: (0, 0))

    def spectra(start, count, rels, four, other):
        height = count * 36 + 8
        cut = halves(count)
        rows = [cut, height - cut] if len(rels) == 1 else [height] * len(rels)
        return pl.pallas_call(
            lambda *refs: spectra_kernel(start, count, rels, *refs),
            out_shape=[jax.ShapeDtypeStruct((n, NM), F32) for n in rows],
            grid_spec=pltpu.PrefetchScalarGridSpec(
                num_scalar_prefetch=2,
                grid=(len(rels), count // 2),
                in_specs=table_specs(start, count, rels) + [kept(192 * count, N2)],
                out_specs=[kept(n, NM) for n in rows],
                scratch_shapes=[pltpu.VMEM((height, NM), F32), pltpu.VMEM((160, N2), F32)],
            ),
            compiler_params=parameters(),
            cost_estimate=cost(5e7 * count * len(rels), 5e5 * count * len(rels)),
            name="spectra",
        )(place, owner, legendre, other, four)

    def implicit(start, count, mine, theirs):
        height = count * 36 + 8
        return pl.pallas_call(
            lambda *refs: implicit_kernel(start, count, *refs),
            out_shape=jax.ShapeDtypeStruct((height, NM), F32),
            grid=(10,),
            in_specs=[smem] * 7 + [pl.BlockSpec((height, N2), lambda t: (0, t))] * 2,
            out_specs=pl.BlockSpec((height, N2), lambda t: (0, t)),
            compiler_params=parameters(),
            cost_estimate=cost(1e7 * count, 6e5 * count),
            name="implicit",
        )(place, owner, *matrices, mine, theirs)

    def grid_rows(start, count, rels, other, blocks):
        height = count * 36 + 8
        return pl.pallas_call(
            lambda *refs: grid_rows_kernel(start, count, rels, *refs),
            out_shape=jax.ShapeDtypeStruct((192 * count, N2), F32),
            grid_spec=pltpu.PrefetchScalarGridSpec(
                num_scalar_prefetch=2,
                grid=(len(rels), count // 2),
                in_specs=table_specs(start, count, rels) + [kept(*b.shape) for b in blocks],
                out_specs=kept(192 * count, N2),
                scratch_shapes=[pltpu.VMEM((height, NM), F32), pltpu.VMEM((160, N2), F32)],
            ),
            compiler_params=parameters(),
            cost_estimate=cost(7e7 * count * len(rels), 5e5 * count * len(rels)),
            name="grid_rows",
        )(place, owner, legendre, other, *blocks)

    def after(value, *earlier):
        return lax.optimization_barrier((value,) + earlier)[0]

    def exchange(value):
        return lax.all_to_all(value, ("core", "wave"), 0, 0, tiled=True)

    steps = [{} for _ in CHUNKS]

    def finish(now, *earlier):
        up, down = now["moving"]
        if earlier:
            up = after(up, *earlier)
        now["sum"] = now["mine"] + up + down
        now["theirs"] = lax.ppermute(now["sum"], "yh", SWAP)

    for k, (start, count) in enumerate(CHUNKS):
        now, before = steps[k], steps[k - 1] if k else None
        now["cut"] = cut = halves(count)
        away, source = aways[k], fours[k]
        if k:
            away = after(away, before["four"])
            source = after(source, before["right"], before["left"])
        now["other"] = lax.ppermute(away, "core", SWAP)
        now["four"] = four = exchange(source).reshape(192 * count, N2)
        top, bottom = spectra(start, count, (2,), four, now["other"])
        right, left, now["mine"] = spectra(start, count, (1, 3, 0), four, now["other"])
        if k:
            finish(before, now["mine"])
            top, bottom, _ = lax.optimization_barrier((top, bottom, before["sum"]))
        top = lax.ppermute(top, "z", UP)
        bottom = lax.ppermute(bottom, "z", DOWN)
        if k:
            right, left = right.at[:cut].add(top), left.at[cut:].add(bottom)
        else:
            right, left = pl.pallas_call(
                fold_kernel,
                out_shape=[jax.ShapeDtypeStruct(right.shape, F32)] * 2,
                in_specs=[whole()] * 4,
                out_specs=[whole()] * 2,
                compiler_params=parameters(),
                cost_estimate=cost(1e5, 1e6),
                name="fold",
            )(right, top, left, bottom)
        now["right"], now["left"] = right, left
        now["moving"] = lax.ppermute(right, "z", UP), lax.ppermute(left, "z", DOWN)
    finish(steps[-1])
    for k, (start, count) in enumerate(CHUNKS):
        now, before = steps[k], steps[k - 1] if k else None
        theirs = after(now["theirs"], *before["ends"]) if k else now["theirs"]
        now["new"] = new = implicit(start, count, now["sum"], theirs)
        upward = after(new, before["top"]) if k else new
        downward = after(new, before["bottom"]) if k else new
        left = lax.ppermute(upward, "z", UP)
        right = lax.ppermute(downward, "z", DOWN)
        now["left"], now["right"] = left, right
        now["ends"] = left[: now["cut"]], right[now["cut"] :]
        now["top"] = lax.ppermute(now["ends"][0], "z", UP)
        now["bottom"] = lax.ppermute(now["ends"][1], "z", DOWN)
    results = []
    for k, (start, count) in enumerate(CHUNKS):
        now = steps[k]
        later = steps[k + 1] if k + 1 < len(CHUNKS) else None
        right, top = now["right"], now["top"]
        if later:
            right = after(right, later["new"])
        rows = grid_rows(start, count, (0, 1, 3), now["other"], (now["new"], right, now["left"]))
        rows = grid_rows(start, count, (2,), now["other"], (top, now["bottom"], rows))
        results.append(exchange(rows.reshape(16, 3, 4 * count, N2)))
    early = pl.pallas_call(
        scatter_kernel,
        out_shape=jax.ShapeDtypeStruct((184, NM), F32),
        in_specs=[whole()] * len(CHUNKS),
        out_specs=whole(),
        compiler_params=parameters(),
        cost_estimate=cost(1e9, 2e6),
        name="scatter",
    )(owner_column, *results[:-1])
    out = pl.pallas_call(
        inverse_kernel,
        out_shape=jax.ShapeDtypeStruct((3, ROWS, 6, NLON), F32),
        in_specs=[whole()] + [smem] * 2 + [whole()] * 4,
        out_specs=whole(),
        scratch_shapes=[pltpu.VMEM((N1, 120, 256), F32), pltpu.VMEM((184, NM), F32)],
        compiler_params=parameters(),
        cost_estimate=cost(4e9, 8e6),
        name="inverse",
    )(owner_column, lat_weights, place, twiddle, backward, early, results[-1])
    return out.transpose(0, 2, 1, 3)


def solution(mesh):
    fine = Mesh(mesh.devices.reshape(2, 4, 2, 8), ("yh", "z", "core", "wave"))
    lat = ("yh", "z", "core")
    rows = P(None, None, lat + ("wave",), None)
    in_specs = (rows, P(), P("wave", lat, None), P(lat), P(), P(), P(), P(), P())
    return jax.shard_map(
        per_device, mesh=fine, in_specs=in_specs, out_specs=rows, check_vma=False
    )
```

```python
import math

import jax
import jax.numpy as jnp
import numpy as np
from jax import lax
from jax.experimental import pallas as pl
from jax.experimental.pallas import tpu as pltpu
from jax.sharding import Mesh, PartitionSpec as P

NLON = 2560
NM = 1280
PAIRS = 640
LAT = 640
PACK = 1408
FL = 18
ROWS = 5
N1 = 20
N2 = 128
HALF = 40
BF = jnp.bfloat16
F32 = jnp.float32
CHUNKS = ((0, 6), (6, 4))
UP = [(i, (i + 1) % 4) for i in range(4)]
DOWN = [(i, (i + 3) % 4) for i in range(4)]
SWAP = [(0, 1), (1, 0)]
VMEM_BYTES = 40 * 1024 * 1024


def split(x):
    high = x.astype(BF)
    return high, (x - high.astype(F32)).astype(BF)


def dot3(x, weight_high, weight_low, dims):
    high, low = split(x)
    out = lax.dot_general(high, weight_high, dims, preferred_element_type=F32)
    out += lax.dot_general(low, weight_high, dims, preferred_element_type=F32)
    return out + lax.dot_general(high, weight_low, dims, preferred_element_type=F32)


NN = (((1,), (0,)), ((), ()))
NT = (((1,), (1,)), ((), ()))


def constant_tables():
    scale = math.sqrt(2.0 / NLON)
    wave1 = np.arange(N1)[:, None]
    lon2 = np.arange(N2)[None, :]
    turn = 2.0 * np.pi * ((wave1 * lon2) % NLON) / NLON
    twiddle = np.stack([np.cos(turn), np.sin(turn)]).astype(np.float32)
    angle = 2.0 * np.pi * ((np.arange(N2)[:, None] * np.arange(64)[None, :]) % N2) / N2
    cos, sin = np.cos(angle) * scale, np.sin(angle) * scale
    zero = np.zeros_like(cos)
    forward = np.concatenate(
        [
            np.concatenate([cos, zero, -sin, zero], 1),
            np.concatenate([sin, zero, cos, zero], 1),
            np.concatenate([zero, cos, zero, -sin], 1),
            np.concatenate([zero, sin, zero, cos], 1),
        ],
        0,
    ).astype(np.float32)
    backward = np.concatenate(
        [
            np.concatenate([cos.T, sin.T, zero.T, zero.T], 1),
            np.concatenate([zero.T, zero.T, cos.T, sin.T], 1),
            np.concatenate([-sin.T, cos.T, zero.T, zero.T], 1),
            np.concatenate([zero.T, zero.T, -sin.T, cos.T], 1),
        ],
        0,
    ).astype(np.float32)

    def parts(table):
        high = table.astype(jnp.bfloat16)
        return np.concatenate([high, (table - high.astype(np.float32)).astype(jnp.bfloat16)])

    return twiddle, parts(forward), parts(backward)


def lane_waves():
    lane = lax.broadcasted_iota(jnp.int32, (1, NM), 1)
    return 2 * (lane // N2) + (lane % N2) // 64 + N1 * (lane % 64)


def one_hot(owner_ref, core, start, rows):
    first = core * HALF + 4 * start
    column = [owner_ref[w * 80 + first : w * 80 + first + rows, :] for w in range(8)]
    column = jnp.concatenate(column, axis=0)[:, 0:1]
    waves = lane_waves()
    second = jnp.where(NM - 1 - column == waves, 1.0, 0.0).astype(BF)
    first = jnp.where(column == waves, 1.0, 0.0).astype(BF)
    return second, first


def fourier_kernel(place_ref, owner_ref, *refs):
    parts = len(CHUNKS)
    sources, table_ref, refs = refs[:3], refs[3], refs[4:]
    send_refs, away_refs = refs[:parts], refs[parts : 2 * parts]
    stage_ref, wide_ref, half_ref, sem = refs[2 * parts : 2 * parts + 4]
    locals_ = refs[2 * parts + 4 :]
    grid_ref, twiddle_ref, weight_ref = locals_
    loads = []
    for k in range(3):
        loads.append(pltpu.make_async_copy(sources[k], locals_[k], sem.at[2 * parts + k]))
        loads[-1].start()
    source = (1 - place_ref[0]) * HALF
    fetches, copies = [], []
    for k, (start, count) in enumerate(CHUNKS):
        rows = pl.ds(4 * start, 4 * count)
        here = table_ref.at[pl.ds(source + 4 * start, 4 * count)]
        fetches.append(pltpu.make_async_copy(here, half_ref.at[rows], sem.at[k]))
        fetches[-1].start()
        copies.append(pltpu.make_async_copy(half_ref.at[rows], away_refs[k], sem.at[parts + k]))
    loads[0].wait()
    loads[1].wait()
    for r in range(ROWS):
        tiles = [grid_ref[:, r, :, N2 * x1 : N2 * (x1 + 1)] for x1 in range(N1)]
        sums = [tiles[x1] + tiles[x1 + 10] for x1 in range(10)]
        differences = [tiles[x1] - tiles[x1 + 10] for x1 in range(10)]
        for m1 in range(11):
            source = sums if m1 % 2 == 0 else differences
            real, imag = source[0], None
            for x1 in range(1, 10):
                turn = 2.0 * math.pi * ((m1 * x1) % N1) / N1
                cos, sin = math.cos(turn), math.sin(turn)
                real = real + source[x1] * cos
                if m1 % 10:
                    term = source[x1] * (-sin)
                    imag = term if imag is None else imag + term
            if imag is None:
                imag = jnp.zeros_like(real)
            for wave, sign in ((m1, 1.0), (N1 - m1, -1.0)):
                if wave in (m1, N1) and sign < 0:
                    continue
                cos = twiddle_ref[0, wave : wave + 1, :]
                sin = twiddle_ref[1, wave : wave + 1, :]
                rotated_real = real * cos + (sign * imag) * sin
                rotated_imag = (sign * imag) * cos - real * sin
                base = (wave % 2) * 256
                rows = slice(3 * r, 3 * r + 3)
                stage_ref[wave // 2, rows, 0:6, base : base + N2] = rotated_real
                stage_ref[wave // 2, rows, 0:6, base + N2 : base + 256] = rotated_imag
    loads[2].wait()
    for fetch, copy in zip(fetches, copies):
        fetch.wait()
        copy.start()
    wide_ref[...] = jnp.zeros_like(wide_ref)
    for t in range(N1 // 2):
        out = dot3(stage_ref[t].reshape(120, 512), weight_ref[:512], weight_ref[512:], NN)
        for r in range(ROWS):
            rows = [out[r * 24 + f * 8 : r * 24 + f * 8 + 6] for f in range(3)]
            both = [row[:, :N2] for row in rows] + [row[:, N2:] for row in rows]
            both = jnp.concatenate(both, axis=0)
            wide_ref[r * 36 : r * 36 + 36, t * N2 : (t + 1) * N2] = both
    high, low = split(wide_ref[...])

    for k, (start, count) in enumerate(CHUNKS):
        group = 4 * count
        for c in range(2):
            half = 8 * group
            picks = jnp.concatenate(one_hot(owner_ref, c, start, group), axis=0)
            out = lax.dot_general(picks, high, NT, preferred_element_type=F32)
            out += lax.dot_general(picks, low, NT, preferred_element_type=F32)
            tile = [out[:half, :180], out[half:, :180], jnp.zeros((half, 24), F32)]
            tile = jnp.concatenate(tile, axis=1)
            for w in range(8):
                for t in range(3):
                    rows = slice(w * group, (w + 1) * group)
                    send_refs[k][c * 8 + w, t] = tile[rows, t * N2 : (t + 1) * N2]
    for copy in copies:
        copy.wait()


def scatter(owner_ref, got_ref, start, count):
    group = 4 * count
    total = jnp.zeros((184, NM), F32)
    for c in range(2):
        second, first = one_hot(owner_ref, c, start, group)
        tiles = [
            jnp.concatenate([got_ref[c * 8 + w, t] for w in range(8)], axis=0) for t in range(3)
        ]
        flipped = jnp.concatenate(tiles, axis=1).T
        for rows, picks in ((flipped[0:184], second), (flipped[180:364], first)):
            high, low = split(rows)
            total += lax.dot_general(high, picks, NN, preferred_element_type=F32)
            total += lax.dot_general(low, picks, NN, preferred_element_type=F32)
    return total


def scatter_kernel(owner_ref, *refs):
    total = jnp.zeros((184, NM), F32)
    for k, (start, count) in enumerate(CHUNKS[:-1]):
        total += scatter(owner_ref, refs[k], start, count)
    refs[-1][...] = total


def inverse_kernel(owner_ref, weight_ref, place_ref, twiddle_ref, table_ref, early_ref, got_ref, out_ref, stage_ref, wide_ref):
    wave = place_ref[1]
    start, count = CHUNKS[-1]
    wide_ref[...] = early_ref[...] + scatter(owner_ref, got_ref, start, count)
    for t in range(N1 // 2):
        rows = []
        for r in range(ROWS):
            block = wide_ref[r * 36 : (r + 1) * 36, t * N2 : (t + 1) * N2]
            block = block * weight_ref[wave * ROWS + r]
            gap = jnp.zeros((2, N2), F32)
            real, imag = [], []
            for f in range(3):
                real += [block[f * 6 : f * 6 + 6], gap]
                imag += [block[FL + f * 6 : FL + f * 6 + 6], gap]
            both = [jnp.concatenate(real, axis=0), jnp.concatenate(imag, axis=0)]
            rows.append(jnp.concatenate(both, axis=1))
        out = dot3(jnp.concatenate(rows, axis=0), table_ref[:256], table_ref[256:], NN)
        for odd in range(2):
            m1 = 2 * t + odd
            real = out[:, odd * 256 : odd * 256 + N2]
            imag = out[:, odd * 256 + N2 : odd * 256 + 256]
            cos = twiddle_ref[0, m1 : m1 + 1, :]
            sin = twiddle_ref[1, m1 : m1 + 1, :]
            stage_ref[m1, :, :N2] = real * cos - imag * sin
            stage_ref[m1, :, N2:] = real * sin + imag * cos
    for r in range(ROWS):
        rows = slice(r * 24, (r + 1) * 24)
        zero, ten = stage_ref[0, rows, :N2], stage_ref[10, rows, :N2]
        sums, gaps = [None], [None]
        for m in range(1, 10):
            sums.append(stage_ref[m, rows, :N2] + stage_ref[N1 - m, rows, :N2])
            gaps.append(stage_ref[m, rows, N2:] - stage_ref[N1 - m, rows, N2:])
        for x1 in range(10):
            even = zero + ten if x1 % 2 == 0 else zero - ten
            odd = jnp.zeros_like(zero)
            for m in range(1, 10):
                turn = 2.0 * math.pi * ((m * x1) % N1) / N1
                term = sums[m] * math.cos(turn) - gaps[m] * math.sin(turn)
                if m % 2 == 0:
                    even = even + term
                else:
                    odd = odd + term
            for f in range(3):
                rows6 = slice(f * 8, f * 8 + 6)
                out_ref[f, r, :, x1 * N2 : (x1 + 1) * N2] = (even + odd)[rows6]
                out_ref[f, r, :, (x1 + 10) * N2 : (x1 + 11) * N2] = (even - odd)[rows6]


def relative(rels, step):
    value = jnp.int32(rels[-1])
    for k, rel in enumerate(rels[:-1]):
        value = jnp.where(step == k, rel, value)
    return value


def spectra_kernel(start, count, rels, place_ref, owner_ref, own_ref, other_ref, four_ref, *refs):
    target, step = pl.program_id(0), pl.program_id(1)
    core, wave = place_ref[0], place_ref[1]
    z = lax.rem(place_ref[2] + relative(rels, target), 4)
    out_refs, work_ref, four_work = refs[:-2], refs[-2], refs[-1]
    extra = count * 36
    group = 4 * count

    @pl.when(step == 0)
    def _():
        work_ref[extra : extra + 8, :] = jnp.zeros((8, NM), F32)

    lane = lax.broadcasted_iota(jnp.int32, (1, NM), 1)
    narrow = lax.broadcasted_iota(jnp.int32, (1, N2), 1)
    kept = []
    for i in range(2):
        first_wave = owner_ref[wave * 80 + core * HALF + 4 * start + z * count + 2 * step + i]
        pair = z * count + 2 * step + i
        for b, band in enumerate((core, 1 - core)):
            base = band * (24 * group) + pair
            tiles = [
                four_ref[pl.ds(base + t * group, 8, stride=3 * group), :] for t in range(3)
            ]
            line = jnp.concatenate(tiles, axis=1)
            for r in range(ROWS):
                pieces = [line[:, r * 36 : r * 36 + 36], jnp.zeros((8, 4), F32)]
                pieces += [line[:, 180 + r * 36 : 216 + r * 36], jnp.zeros((8, 52), F32)]
                piece = jnp.concatenate(pieces, axis=1)
                four_work[pl.ds(i * 80 + b * HALF + r, 8, stride=ROWS), :] = piece
        four = four_work[i * 80 : (i + 1) * 80, :]
        four_high = four.astype(BF).astype(F32)
        left = jnp.concatenate([four_high, four_high, four - four_high], axis=0).T
        table = jnp.concatenate([own_ref[i], other_ref[i]], axis=0)
        main = table[:, :NM]
        main_high = main.astype(BF).astype(F32)
        right = jnp.concatenate([main_high, main - main_high, main_high], axis=0)
        both = lax.dot_general(left[:80].astype(BF), right.astype(BF), NN, preferred_element_type=F32)
        kept.append(jnp.where(lane < NM - first_wave, both[40:80], both[0:40])[:36])
        last = jnp.sum(table[:, NM : NM + 1] * four, axis=0, keepdims=True)
        spot = pl.multiple_of((2 * step + i) * N2, N2)
        work_ref[extra : extra + 1, pl.ds(spot, N2)] = jnp.where(narrow < 36, last, 0.0)
    work_ref[pl.ds(pl.multiple_of(step * 72, 8), 72), :] = jnp.concatenate(kept, axis=0)

    @pl.when(step == count // 2 - 1)
    def _():
        if len(rels) == 1:
            cut = halves(count)
            out_refs[0][...] = work_ref[:cut]
            out_refs[1][...] = work_ref[cut:]
        else:
            for k, out_ref in enumerate(out_refs):

                @pl.when(target == k)
                def _(out_ref=out_ref):
                    out_ref[...] = work_ref[...]


def halves(count):
    return (count * 36 + 8) // 16 * 8


def implicit_rows(load, degree, modes_e, modes_f, rates, height, heating):
    q = degree * (degree + 1.0) / float(NM * (NM + 1))
    rotation = 1.0 / (1.0 + 4.0 * q * q)
    damping = [1.0 / (1.0 + 4.0 * q * rates[i]) for i in range(6)]
    out = []
    for part in range(2):
        base = part * FL
        d = [load(base + 6 + l) for l in range(6)]
        t = [load(base + 12 + l) for l in range(6)]
        forced = []
        for l in range(6):
            total = d[l]
            for h in range(6):
                total = total - heating[h * 6 + l] * t[h]
            forced.append(total)
        modal = []
        for i in range(6):
            total = modes_e[i] * forced[0]
            for h in range(1, 6):
                total = total + modes_e[h * 6 + i] * forced[h]
            modal.append(total * damping[i])
        spread = []
        for l in range(6):
            total = modes_f[l] * modal[0]
            for i in range(1, 6):
                total = total + modes_f[i * 6 + l] * modal[i]
            spread.append(total)
        out += [load(base + l) * rotation for l in range(6)]
        out += spread
        for l in range(6):
            total = height[l] * spread[0]
            for h in range(1, 6):
                total = total + height[h * 6 + l] * spread[h]
            out.append(t[l] - q * total)
    return out


def implicit_kernel(start, count, place_ref, owner_ref, e_ref, f_ref, rate_ref, height_ref, heat_ref, x_ref, y_ref, out_ref):
    core, wave, z = place_ref[0], place_ref[1], place_ref[2]
    matrices = [[ref[i] for i in range(36)] for ref in (e_ref, f_ref)]
    rates = [rate_ref[i] for i in range(6)]
    heights = [[ref[i] for i in range(36)] for ref in (height_ref, heat_ref)]
    arguments = (matrices[0], matrices[1], rates, heights[0], heights[1])
    row = lax.broadcasted_iota(jnp.int32, (count, 1), 0)
    first_wave = jnp.zeros((count, 1), jnp.int32)
    for i in range(count):
        value = owner_ref[wave * 80 + core * HALF + 4 * start + z * count + i]
        first_wave = jnp.where(row == i, value, first_wave)

    tile = pl.program_id(0)
    packed = tile * N2 + lax.broadcasted_iota(jnp.int32, (count, N2), 1)
    degree = jnp.where(packed < NM - first_wave, first_wave + packed, packed - 1).astype(F32)

    def load(j):
        spot = pl.ds(j, count, stride=36)
        return x_ref[spot, :] + y_ref[spot, :]

    for j, value in enumerate(implicit_rows(load, degree, *arguments)):
        out_ref[pl.ds(j, count, stride=36), :] = value
    extra = count * 36
    line = x_ref[extra : extra + 1, :] + y_ref[extra : extra + 1, :]
    flipped = jnp.broadcast_to(line, (8, N2)).T
    degree = jnp.full((1, 8), NM - 1.0, F32)
    values = implicit_rows(lambda j: flipped[j : j + 1], degree, *arguments)
    values.append(jnp.zeros((N2 - 36, 8), F32))
    out_ref[extra : extra + 8, :] = jnp.concatenate(values, axis=0).T


def grid_rows_kernel(start, count, rels, place_ref, owner_ref, own_ref, other_ref, *refs):
    target, step = pl.program_id(0), pl.program_id(1)
    core, wave = place_ref[0], place_ref[1]
    z = lax.rem(place_ref[2] + relative(rels, target), 4)
    out_ref, work_ref, back_work = refs[-3:]
    if len(rels) == 1:
        top_ref, bottom_ref, before_ref = refs[:-3]
    else:
        spec_refs = refs[:-3]
    extra = count * 36
    group = 4 * count
    cut = halves(count)

    for k in range(len(rels)):

        @pl.when((target == k) & (step == 0))
        def _(k=k):
            if len(rels) == 1:
                work_ref[:cut] = top_ref[...]
                work_ref[cut:] = bottom_ref[...]
                out_ref[...] = before_ref[...]
            else:
                work_ref[...] = spec_refs[k][...]

    lane = lax.broadcasted_iota(jnp.int32, (1, NM), 1)
    block = work_ref[pl.ds(pl.multiple_of(step * 72, 8), 72), :]
    pad = jnp.zeros((4, NM), F32)
    for i in range(2):
        first_wave = owner_ref[wave * 80 + core * HALF + 4 * start + z * count + 2 * step + i]
        pair = z * count + 2 * step + i
        values = jnp.concatenate([block[i * 36 : i * 36 + 36], pad], axis=0)
        is_first = lane < NM - first_wave
        both = jnp.concatenate(
            [jnp.where(is_first, 0.0, values), jnp.where(is_first, values, 0.0)], axis=0
        )
        high, low = split(both)
        table = jnp.concatenate([own_ref[i], other_ref[i]], axis=0)
        back = dot3(table[:, :NM], high, low, NT)
        back = jnp.concatenate([back, jnp.zeros((80, 48), F32)], axis=1)
        spot = pl.multiple_of((2 * step + i) * N2, N2)
        last = work_ref[extra : extra + 1, pl.ds(spot, N2)]
        back = back + table[:, NM : NM + 1] * last
        back_work[i * 80 : (i + 1) * 80, :] = back
        for b, band in enumerate((core, 1 - core)):
            rows = [
                back_work[pl.ds(i * 80 + b * HALF + r, 8, stride=ROWS), :] for r in range(ROWS)
            ]
            line = [row[:, 0:36] for row in rows] + [row[:, 40:76] for row in rows]
            line = jnp.concatenate(line + [jnp.zeros((8, 24), F32)], axis=1)
            base = band * (24 * group) + pair
            for t in range(3):
                spot = pl.ds(base + t * group, 8, stride=3 * group)
                out_ref[spot, :] = line[:, t * N2 : (t + 1) * N2]


def fold_kernel(right_ref, top_ref, left_ref, bottom_ref, right_out, left_out):
    cut = top_ref.shape[0]
    right_out[:cut] = right_ref[:cut] + top_ref[...]
    right_out[cut:] = right_ref[cut:]
    left_out[:cut] = left_ref[:cut]
    left_out[cut:] = left_ref[cut:] + bottom_ref[...]


def sum_kernel(x_ref, y_ref, z_ref, out_ref):
    out_ref[...] = x_ref[...] + y_ref[...] + z_ref[...]


def parameters():
    return pltpu.CompilerParams(vmem_limit_bytes=VMEM_BYTES)


def whole(space=pltpu.VMEM):
    return pl.BlockSpec(memory_space=space)


def cost(flops, size):
    return pl.CostEstimate(flops=int(flops), bytes_accessed=int(size), transcendentals=0)


def per_device(
    grad_grid, owner, legendre, lat_weights, modes_e, modes_f, rates, height_matrix, heating_matrix
):
    core, wave, z = lax.axis_index("core"), lax.axis_index("wave"), lax.axis_index("z")
    twiddle, forward, backward = constant_tables()
    smem = whole(pltpu.SMEM)
    place = jnp.stack([core, wave, z]).astype(jnp.int32)
    owner_column = jnp.broadcast_to(owner[:, None], (PAIRS, N2))
    matrices = [m.reshape(36) for m in (modes_e, modes_f)] + [rates]
    matrices += [m.reshape(36) for m in (height_matrix, heating_matrix)]

    made = pl.pallas_call(
        fourier_kernel,
        out_shape=[jax.ShapeDtypeStruct((16, 3, 4 * n, N2), F32) for _, n in CHUNKS]
        + [jax.ShapeDtypeStruct((4 * n, HALF, PACK), F32) for _, n in CHUNKS],
        in_specs=[smem, whole()] + [whole(pltpu.HBM)] * 4,
        out_specs=[whole()] * len(CHUNKS) + [whole(pltpu.HBM)] * len(CHUNKS),
        scratch_shapes=[
            pltpu.VMEM((10, 15, 8, 512), F32),
            pltpu.VMEM((184, NM), F32),
            pltpu.VMEM((HALF, HALF, PACK), F32),
            pltpu.SemaphoreType.DMA((2 * len(CHUNKS) + 3,)),
            pltpu.VMEM((3, ROWS, 6, NLON), F32),
            pltpu.VMEM((2, N1, N2), F32),
            pltpu.VMEM((1024, 256), BF),
        ],
        compiler_params=parameters(),
        cost_estimate=cost(4e9, 2.6e7),
        name="fourier",
    )(place, owner_column, grad_grid.transpose(0, 2, 1, 3), twiddle, forward, legendre)
    fours, aways = made[: len(CHUNKS)], made[len(CHUNKS) :]

    def zone(rels, t, place):
        return lax.rem(place[2] + relative(rels, t), 4)

    def table_specs(start, count, rels):
        return [
            pl.BlockSpec(
                (2, HALF, PACK),
                lambda t, s, place, owner: (
                    place[0] * 20 + 2 * start + zone(rels, t, place) * (count // 2) + s,
                    0,
                    0,
                ),
            ),
            pl.BlockSpec(
                (2, HALF, PACK),
                lambda t, s, place, owner: (zone(rels, t, place) * (count // 2) + s, 0, 0),
            ),
        ]

    def kept(rows, lanes):
        return pl.BlockSpec((rows, lanes), lambda t, s, place, owner: (0, 0))

    def spectra(start, count, rels, four, other):
        height = count * 36 + 8
        cut = halves(count)
        rows = [cut, height - cut] if len(rels) == 1 else [height] * len(rels)
        return pl.pallas_call(
            lambda *refs: spectra_kernel(start, count, rels, *refs),
            out_shape=[jax.ShapeDtypeStruct((n, NM), F32) for n in rows],
            grid_spec=pltpu.PrefetchScalarGridSpec(
                num_scalar_prefetch=2,
                grid=(len(rels), count // 2),
                in_specs=table_specs(start, count, rels) + [kept(192 * count, N2)],
                out_specs=[kept(n, NM) for n in rows],
                scratch_shapes=[pltpu.VMEM((height, NM), F32), pltpu.VMEM((160, N2), F32)],
            ),
            compiler_params=parameters(),
            cost_estimate=cost(5e7 * count * len(rels), 5e5 * count * len(rels)),
            name="spectra",
        )(place, owner, legendre, other, four)

    def implicit(start, count, mine, theirs):
        height = count * 36 + 8
        return pl.pallas_call(
            lambda *refs: implicit_kernel(start, count, *refs),
            out_shape=jax.ShapeDtypeStruct((height, NM), F32),
            grid=(10,),
            in_specs=[smem] * 7 + [pl.BlockSpec((height, N2), lambda t: (0, t))] * 2,
            out_specs=pl.BlockSpec((height, N2), lambda t: (0, t)),
            compiler_params=parameters(),
            cost_estimate=cost(1e7 * count, 6e5 * count),
            name="implicit",
        )(place, owner, *matrices, mine, theirs)

    def grid_rows(start, count, rels, other, blocks):
        height = count * 36 + 8
        return pl.pallas_call(
            lambda *refs: grid_rows_kernel(start, count, rels, *refs),
            out_shape=jax.ShapeDtypeStruct((192 * count, N2), F32),
            grid_spec=pltpu.PrefetchScalarGridSpec(
                num_scalar_prefetch=2,
                grid=(len(rels), count // 2),
                in_specs=table_specs(start, count, rels) + [kept(*b.shape) for b in blocks],
                out_specs=kept(192 * count, N2),
                scratch_shapes=[pltpu.VMEM((height, NM), F32), pltpu.VMEM((160, N2), F32)],
            ),
            compiler_params=parameters(),
            cost_estimate=cost(7e7 * count * len(rels), 5e5 * count * len(rels)),
            name="grid_rows",
        )(place, owner, legendre, other, *blocks)

    def after(value, *earlier):
        return lax.optimization_barrier((value,) + earlier)[0]

    def exchange(value):
        return lax.all_to_all(value, ("core", "wave"), 0, 0, tiled=True)

    steps = [{} for _ in CHUNKS]

    def finish(now, *earlier):
        up, down = now["moving"]
        if earlier:
            up = after(up, *earlier)
        now["sum"] = now["mine"] + up + down
        now["theirs"] = lax.ppermute(now["sum"], "yh", SWAP)

    for k, (start, count) in enumerate(CHUNKS):
        now, before = steps[k], steps[k - 1] if k else None
        now["cut"] = cut = halves(count)
        away, source = aways[k], fours[k]
        if k:
            away = after(away, before["four"])
            source = after(source, before["right"], before["left"])
        now["other"] = lax.ppermute(away, "core", SWAP)
        now["four"] = four = exchange(source).reshape(192 * count, N2)
        top, bottom = spectra(start, count, (2,), four, now["other"])
        right, left, now["mine"] = spectra(start, count, (1, 3, 0), four, now["other"])
        if k:
            finish(before, now["mine"])
            top, bottom, _ = lax.optimization_barrier((top, bottom, before["sum"]))
        top = lax.ppermute(top, "z", UP)
        bottom = lax.ppermute(bottom, "z", DOWN)
        if k:
            right, left = right.at[:cut].add(top), left.at[cut:].add(bottom)
        else:
            right, left = pl.pallas_call(
                fold_kernel,
                out_shape=[jax.ShapeDtypeStruct(right.shape, F32)] * 2,
                in_specs=[whole()] * 4,
                out_specs=[whole()] * 2,
                compiler_params=parameters(),
                cost_estimate=cost(1e5, 1e6),
                name="fold",
            )(right, top, left, bottom)
        now["right"], now["left"] = right, left
        now["moving"] = lax.ppermute(right, "z", UP), lax.ppermute(left, "z", DOWN)
    finish(steps[-1])
    for k, (start, count) in enumerate(CHUNKS):
        now, before = steps[k], steps[k - 1] if k else None
        theirs = after(now["theirs"], *before["ends"]) if k else now["theirs"]
        now["new"] = new = implicit(start, count, now["sum"], theirs)
        if k:
            new = after(new, before["top"], before["bottom"])
        left = lax.ppermute(new, "z", UP)
        right = lax.ppermute(new, "z", DOWN)
        now["left"], now["right"] = left, right
        now["ends"] = left[: now["cut"]], right[now["cut"] :]
        now["top"] = lax.ppermute(now["ends"][0], "z", UP)
        now["bottom"] = lax.ppermute(now["ends"][1], "z", DOWN)
    results = []
    for k, (start, count) in enumerate(CHUNKS):
        now = steps[k]
        later = steps[k + 1] if k + 1 < len(CHUNKS) else None
        right, top = now["right"], now["top"]
        if later:
            right = after(right, later["new"])
        rows = grid_rows(start, count, (0, 1, 3), now["other"], (now["new"], right, now["left"]))
        rows = grid_rows(start, count, (2,), now["other"], (top, now["bottom"], rows))
        if later:
            rows = after(rows, *later["ends"])
        results.append(exchange(rows.reshape(16, 3, 4 * count, N2)))
    early = pl.pallas_call(
        scatter_kernel,
        out_shape=jax.ShapeDtypeStruct((184, NM), F32),
        in_specs=[whole()] * len(CHUNKS),
        out_specs=whole(),
        compiler_params=parameters(),
        cost_estimate=cost(1e9, 2e6),
        name="scatter",
    )(owner_column, *results[:-1])
    out = pl.pallas_call(
        inverse_kernel,
        out_shape=jax.ShapeDtypeStruct((3, ROWS, 6, NLON), F32),
        in_specs=[whole()] + [smem] * 2 + [whole()] * 4,
        out_specs=whole(),
        scratch_shapes=[pltpu.VMEM((N1, 120, 256), F32), pltpu.VMEM((184, NM), F32)],
        compiler_params=parameters(),
        cost_estimate=cost(4e9, 8e6),
        name="inverse",
    )(owner_column, lat_weights, place, twiddle, backward, early, results[-1])
    return out.transpose(0, 2, 1, 3)


def solution(mesh):
    fine = Mesh(mesh.devices.reshape(2, 4, 2, 8), ("yh", "z", "core", "wave"))
    lat = ("yh", "z", "core")
    rows = P(None, None, lat + ("wave",), None)
    in_specs = (rows, P(), P("wave", lat, None), P(lat), P(), P(), P(), P(), P())
    return jax.shard_map(
        per_device, mesh=fine, in_specs=in_specs, out_specs=rows, check_vma=False
    )
```
